256 devices in a mesh: dp: 16 (over x_hi, y, core), tensor: 16 (over x_lo, z).
Axes of the slice: x: 4 (x_hi: 2, x_lo: 2; x = x_hi * 2 + x_lo), y: 4, z: 8, core: 2. Of those that a mesh axis runs over, the one named last changes fastest.
Arguments:
- inputs: bfloat16 [2048, 8192], P(('dp', 'tensor')), may hold values from -24 to 24
- out_grad: bfloat16 [2048, 8192], P(('dp', 'tensor')), may hold values from -16 to 16
- gate_pre: bfloat16 [2048, 16384], P('dp', 'tensor'), may hold values from -6 to 6
- up_pre: bfloat16 [2048, 16384], P('dp', 'tensor'), may hold values from -6 to 6
- gate_weight: bfloat16 [8192, 16384], P('dp', 'tensor'), may hold values from -0.0625 to 0.0625
- up_weight: bfloat16 [8192, 16384], P('dp', 'tensor'), may hold values from -0.0625 to 0.0625
- down_weight: bfloat16 [16384, 8192], P('tensor', 'dp'), may hold values from -0.046875 to 0.046875
Outputs:
- input_grad: bfloat16 [16, 128, 8192], P(None, 'tensor', 'dp')
- gate_grad: float32 [8192, 16384], P('dp', 'tensor')
- up_grad: float32 [8192, 16384], P('dp', 'tensor')
- down_grad: float32 [16384, 8192], P('tensor', 'dp')
The draws below stay inside these ranges and needn't reach their ends.
All inputs are finite; a program needn't handle non-finite values.
Results may differ from the reference program's by a relative error of at most 0.005.
Values may be sent and summed in bfloat16 or wider, within the bound.
No kernel may reach another device: no remote copies, remote signals or barrier semaphores. Data moves between devices by JAX's collectives and lax.ppermute only.
A program may use at most 128 MiB of HBM per device.

```python
import jax
import jax.numpy as jnp

D = 8192
FF_WIN = 16384
TOK_GROUP = 128
TOKENS = 2048
N_DP = 16


def draw_inputs(key, part):
    key = jax.random.fold_in(key, 5)
    noise_key, row_key, col_key = jax.random.split(key, 3)
    noise = jax.random.normal(noise_key, (TOKENS, D), jnp.float32)
    row_scale = jax.random.uniform(row_key, (TOKENS, 1), jnp.float32, 0.5, 2.0)
    col_scale = jax.random.uniform(col_key, (1, D), jnp.float32, 0.5, 2.0)
    values = noise * row_scale * col_scale
    return jnp.clip(values, -24.0, 24.0).astype(jnp.bfloat16)


def draw_out_grad(key, part):
    key = jax.random.fold_in(key, 9)
    noise_key, row_key = jax.random.split(key, 2)
    noise = jax.random.normal(noise_key, (TOKENS, D), jnp.float32)
    row_scale = jax.random.uniform(row_key, (TOKENS, 1), jnp.float32, 0.5, 2.0)
    values = noise * row_scale
    return jnp.clip(values, -16.0, 16.0).astype(jnp.bfloat16)


def level_of(stream_key, shape, cuts, least, top_value):
    level, own = 1.0, jax.random.fold_in(stream_key, 6)
    for axis_at, parts in cuts:
        heights = jnp.exp(jax.random.uniform(jax.random.fold_in(own, axis_at), (parts,), jnp.float32, least / len(cuts), top_value / len(cuts)))
        level = level * jnp.repeat(heights, shape[axis_at] // parts).reshape([-1 if axis == axis_at else 1 for axis in range(len(shape))])
    return level


def gaussian(stream_key, dims, scale, reach, cuts=(), dtype=jnp.bfloat16):
    array = jax.random.normal(stream_key, dims, jnp.float32) * scale
    if len(cuts) > 0:
        array = level_of(stream_key, dims, cuts, -0.22, 0.18) * array
    return jnp.clip(array, min=-reach, max=reach).astype(dtype)


def setup_inputs(seed: int = 0) -> dict:
    key_list = jax.random.split(jax.random.key(seed), 8)
    return {
        "inputs": draw_inputs(jax.random.fold_in(key_list[7], 71), 0),
        "out_grad": draw_out_grad(jax.random.fold_in(key_list[7], 71), 0),
        "gate_pre": gaussian(key_list[2], (TOKENS, FF_WIN), 1.0, 6.0, ((0, 16), (1, 16))),
        "up_pre": gaussian(key_list[3], (TOKENS, FF_WIN), 1.0, 6.0, ((0, 16), (1, 16))),
        "gate_weight": gaussian(key_list[4], (D, FF_WIN), D ** -0.5, 0.0625, ((0, 16), (1, 16))),
        "up_weight": gaussian(key_list[5], (D, FF_WIN), D ** -0.5, 0.0625, ((0, 16), (1, 16))),
        "down_weight": gaussian(key_list[6], (FF_WIN, D), FF_WIN ** -0.5, 0.046875, ((0, 16), (1, 16))),
    }


def reference(inputs, out_grad, gate_pre, up_pre, gate_weight, up_weight, down_weight):
    grad_hidden = jnp.dot(out_grad, down_weight.T, preferred_element_type=jnp.float32)
    gate_values = gate_pre.astype(jnp.float32)
    up_values = up_pre.astype(jnp.float32)
    sigmoid = jax.nn.sigmoid(gate_values)
    activated = gate_values * sigmoid
    hidden = (activated * up_values).astype(jnp.bfloat16)
    grad_gate = (grad_hidden * up_values * sigmoid * (1.0 + gate_values * (1.0 - sigmoid))).astype(jnp.bfloat16)
    grad_up = (grad_hidden * activated).astype(jnp.bfloat16)
    down_grad = jnp.dot(hidden.T, out_grad, preferred_element_type=jnp.float32)
    gate_grad = jnp.dot(inputs.T, grad_gate, preferred_element_type=jnp.float32)
    up_grad = jnp.dot(inputs.T, grad_up, preferred_element_type=jnp.float32)
    input_rows = jnp.dot(grad_gate, gate_weight.T, preferred_element_type=jnp.float32) + jnp.dot(grad_up, up_weight.T, preferred_element_type=jnp.float32)
    input_grad = input_rows.astype(jnp.bfloat16).reshape(N_DP, TOK_GROUP, D)
    return input_grad, gate_grad, up_grad, down_grad
```

```python
import jax
import jax.numpy as jnp
from jax import lax
from jax.sharding import Mesh, PartitionSpec as P

BF16 = jnp.bfloat16
F32 = jnp.float32
CHIPS = ("xh", "y")


def swap(value, axis):
    return lax.ppermute(value, axis, [(0, 1), (1, 0)])


def shift(value, axis, by):
    size = lax.axis_size(axis)
    return lax.ppermute(value, axis, [(i, (i + by) % size) for i in range(size)])


def after(value, *others):
    return lax.optimization_barrier((value, *others))[0]


def ring_gather(own):
    rows = own.shape[1]
    half = rows // 2
    right, left = [own], [own]
    for _ in range(3):
        right.append(shift(right[-1], "z", 1))
        left.append(shift(left[-1], "z", -1))
    far_right = shift(right[3][:, :half], "z", 1)
    far_left = shift(left[3][:, half:], "z", -1)
    parts = left + [far_right, far_left] + right[:0:-1]
    return jnp.concatenate(parts, axis=1), (far_right, far_left)


def ring_scatter(blocks):
    half = blocks.shape[2] // 2
    right = shift(blocks[:, 4, :half].astype(BF16), "z", 1)
    left = shift(blocks[:, 4, half:].astype(BF16), "z", -1)
    for k in (3, 2, 1):
        mine, other = blocks[:, k], blocks[:, 8 - k]
        if k == 3:
            mine = jnp.concatenate([mine[:, :half] + right.astype(F32), mine[:, half:]], axis=1)
            other = jnp.concatenate([other[:, :half], other[:, half:] + left.astype(F32)], axis=1)
        else:
            mine = mine + right.astype(F32)
            other = other + left.astype(F32)
        if k > 1:
            mine, other = mine.astype(BF16), other.astype(BF16)
        right, left = shift(mine, "z", 1), shift(other, "z", -1)
    return blocks[:, 0] + right + left


def contract_rows(left, right):
    return lax.dot_general(left, right, (((0,), (0,)), ((), ())), preferred_element_type=F32)


def against_weight(left, weight):
    return lax.dot_general(left, weight, (((1,), (1,)), ((), ())), preferred_element_type=F32)


def shards(inputs, out_grad, gate_pre, up_pre, gate_weight, up_weight, down_weight):
    core, x_lo, z = lax.axis_index("c"), lax.axis_index("xl"), lax.axis_index("z")
    rows = inputs.shape[0]
    chips = lax.axis_size(CHIPS)
    ring = lax.axis_size("z")
    wide = inputs.shape[1] // chips
    narrow = wide // 2
    units = gate_pre.shape[1]

    def by_chip(value):
        return value.reshape(rows, chips, wide).transpose(1, 0, 2)

    both = jnp.concatenate([by_chip(out_grad), by_chip(inputs)], axis=1)
    both = lax.all_to_all(both, CHIPS, split_axis=0, concat_axis=0, tiled=True)
    both = jnp.where(core == 0, both, jnp.roll(both, narrow, axis=2))

    def nearest_first(value):
        value = value.reshape(2, ring, rows, units)
        value = jnp.where(x_lo == 0, value, value[::-1])
        value = lax.dynamic_slice_in_dim(jnp.concatenate([value, value], axis=1), z, ring, axis=1)
        return value.transpose(1, 0, 2, 3).reshape(ring * 2 * rows, units)

    gate_all = lax.all_gather(nearest_first(gate_pre), CHIPS, axis=0, tiled=True)
    up_all = lax.all_gather(nearest_first(up_pre), CHIPS, axis=0, tiled=True)

    down_pair = jnp.concatenate([down_weight, swap(down_weight, "c")], axis=1)
    gate_pair = jnp.concatenate([gate_weight, swap(gate_weight, "c")], axis=0)
    up_pair = jnp.concatenate([up_weight, swap(up_weight, "c")], axis=0)

    own_grad, own_in = both[:, :rows], both[:, rows:]
    own_grad = jnp.concatenate([own_grad, swap(own_grad, "xl")], axis=1)
    grad_cols, last = ring_gather(own_grad)
    own_in = after(own_in, *last)
    own_in = jnp.concatenate([own_in, swap(own_in, "xl")], axis=1)
    in_cols, _ = ring_gather(own_in)
    tokens = grad_cols.shape[0] * grad_cols.shape[1]
    grad_cols = grad_cols.reshape(tokens, wide)
    in_cols = in_cols.reshape(tokens, wide)

    part = against_weight(grad_cols, down_pair).astype(BF16).reshape(chips, tokens // chips, units)
    part = lax.all_to_all(part, CHIPS, split_axis=0, concat_axis=0, tiled=True)
    grad_hidden = jnp.sum(part.astype(F32), axis=0).astype(BF16)
    grad_hidden = jnp.broadcast_to(grad_hidden[None], part.shape)
    grad_hidden = lax.all_to_all(grad_hidden, CHIPS, split_axis=0, concat_axis=0, tiled=True)
    grad_hidden = grad_hidden.reshape(tokens, units).astype(F32)

    gate_values, up_values = gate_all.astype(F32), up_all.astype(F32)
    sigmoid = jax.nn.sigmoid(gate_values)
    activated = gate_values * sigmoid
    hidden = (activated * up_values).astype(BF16)
    grad_gate = (grad_hidden * up_values * sigmoid * (1.0 + gate_values * (1.0 - sigmoid))).astype(BF16)
    grad_up = (grad_hidden * activated).astype(BF16)

    in_part = against_weight(grad_gate, gate_pair) + against_weight(grad_up, up_pair)
    summed = ring_scatter(in_part.reshape(chips, ring, 2 * rows, wide))
    summed = summed[:, :rows] + swap(summed[:, rows:], "xl")
    summed = summed.astype(BF16)
    mine, other = summed[:, :, :narrow], swap(summed[:, :, narrow:], "c")
    first, second = jnp.where(core == 0, mine, other), jnp.where(core == 0, other, mine)
    input_grad = jnp.stack([first, second], axis=1).reshape(2 * chips, rows, narrow)

    down_grad = contract_rows(hidden, grad_cols[:, :narrow]) + swap(
        contract_rows(hidden, grad_cols[:, narrow:]), "c"
    )
    gate_grad = contract_rows(in_cols[:, :narrow], grad_gate) + swap(
        contract_rows(in_cols[:, narrow:], grad_gate), "c"
    )
    up_grad = contract_rows(in_cols[:, :narrow], grad_up) + swap(
        contract_rows(in_cols[:, narrow:], grad_up), "c"
    )
    return (input_grad, gate_grad, up_grad, down_grad)


def solution(mesh):
    grid = Mesh(mesh.devices.reshape(2, 4, 2, 2, 8), ("xh", "y", "c", "xl", "z"))
    dp, tensor = ("xh", "y", "c"), ("xl", "z")
    in_specs = (
        P(dp + tensor, None),
        P(dp + tensor, None),
        P(dp, tensor),
        P(dp, tensor),
        P(dp, tensor),
        P(dp, tensor),
        P(tensor, dp),
    )
    out_specs = (P(None, tensor, dp), P(dp, tensor), P(dp, tensor), P(tensor, dp))
    return jax.shard_map(shards, mesh=grid, in_specs=in_specs, out_specs=out_specs, check_vma=False)
```

```python
import jax
import jax.numpy as jnp
from jax import lax
from jax.sharding import Mesh, PartitionSpec as P

BF16 = jnp.bfloat16
F32 = jnp.float32
CHIPS = ("xh", "y")


def swap(value, axis):
    return lax.ppermute(value, axis, [(0, 1), (1, 0)])


def shift(value, axis, by):
    size = lax.axis_size(axis)
    return lax.ppermute(value, axis, [(i, (i + by) % size) for i in range(size)])


def after(value, *others):
    return lax.optimization_barrier((value, *others))[0]


def ring_blocks(own):
    half = own.shape[0] // 2
    right, left = [own], [own]
    for _ in range(3):
        right.append(shift(right[-1], "z", 1))
        left.append(shift(left[-1], "z", -1))
    far = (shift(right[3][:half], "z", 1), shift(left[3][half:], "z", -1))
    return left, far, right


def in_order(left, far, right):
    far = jnp.concatenate(far, axis=0)
    return left + [far] + right[:0:-1]


def chip_gather(own):
    rows = own.shape[0]
    x_hi, y = lax.axis_index("xh"), lax.axis_index("y")
    other = swap(own, "xh")
    right = [shift(own, "y", 1), shift(other, "y", 1)]
    left = [shift(own, "y", -1), shift(other, "y", -1)]
    far = [shift(right[0], "y", 1), shift(left[1], "y", -1)]
    whole = jnp.zeros((8 * rows, own.shape[1]), own.dtype)
    for by, pair in ((0, (own, other)), (3, right), (1, left), (2, far)):
        for flip, block in enumerate(pair):
            place = (x_hi ^ flip) * 4 + lax.rem(y + by, 4)
            whole = lax.dynamic_update_slice_in_dim(whole, block, place * rows, axis=0)
    return whole


def contract_rows(left, right):
    return lax.dot_general(left, right, (((0,), (0,)), ((), ())), preferred_element_type=F32)


def against_weight(left, weight):
    return lax.dot_general(left, weight, (((1,), (1,)), ((), ())), preferred_element_type=F32)


def shards(inputs, out_grad, gate_pre, up_pre, gate_weight, up_weight, down_weight):
    core, x_lo, z = lax.axis_index("c"), lax.axis_index("xl"), lax.axis_index("z")
    rows = inputs.shape[0]
    chips = lax.axis_size(CHIPS)
    ring = lax.axis_size("z")
    wide = inputs.shape[1] // chips
    narrow = wide // 2
    units = gate_pre.shape[1]

    def by_chip(value):
        return value.reshape(rows, chips, wide).transpose(1, 0, 2)

    both = jnp.concatenate([by_chip(out_grad), by_chip(inputs)], axis=1)
    gate_pre, up_pre, both = lax.optimization_barrier((gate_pre, up_pre, both))
    both = lax.all_to_all(both, CHIPS, split_axis=0, concat_axis=0, tiled=True)
    both = jnp.where(core == 0, both, jnp.roll(both, narrow, axis=2))

    def nearest_first(value):
        value = value.reshape(2, ring, rows, units)
        value = jnp.where(x_lo == 0, value, value[::-1])
        value = lax.dynamic_slice_in_dim(jnp.concatenate([value, value], axis=1), z, ring, axis=1)
        return value.reshape(2 * ring * rows, units)

    gate_all = lax.all_gather(nearest_first(gate_pre), CHIPS, axis=0, tiled=True)
    up_all = chip_gather(nearest_first(up_pre))

    down_pair = jnp.concatenate([down_weight, swap(down_weight, "c")], axis=1)
    gate_pair = jnp.concatenate([gate_weight, swap(gate_weight, "c")], axis=0)
    up_pair = jnp.concatenate([up_weight, swap(up_weight, "c")], axis=0)

    own_grad, own_in = both[:, :rows], both[:, rows:]
    left, far, right = ring_blocks(own_grad)
    mine = in_order(left, far, right)
    crossed = [[swap(b, "xl") for b in blocks] for blocks in (left, far, right[1:])]
    other = in_order(crossed[0], crossed[1], [None, *crossed[2]])
    grad_cols = jnp.concatenate(mine + other, axis=1)

    own_in = after(own_in, *far)
    own_in = jnp.concatenate([own_in, swap(both[:, rows:], "xl")], axis=1)
    blocks = in_order(*ring_blocks(own_in))
    in_cols = jnp.concatenate([b[:, :rows] for b in blocks] + [b[:, rows:] for b in blocks], axis=1)

    share = grad_cols.shape[1]
    tokens = chips * share
    grad_cols = grad_cols.reshape(tokens, wide)
    in_cols = in_cols.reshape(tokens, wide)

    part = against_weight(grad_cols, down_pair).astype(BF16).reshape(chips, share, units)
    part = lax.all_to_all(part, CHIPS, split_axis=0, concat_axis=0, tiled=True)
    grad_hidden = jnp.sum(part.astype(F32), axis=0).astype(BF16)

    def halves(value):
        value = value.reshape(chips, 2, share // 2, units)
        return value[:, 0].reshape(tokens // 2, units), value[:, 1].reshape(tokens // 2, units)

    def spread(value):
        value = jnp.broadcast_to(value[None], (chips, *value.shape))
        value = lax.all_to_all(value, CHIPS, split_axis=0, concat_axis=0, tiled=True)
        return value.reshape(tokens // 2, units)

    def back(grad_hidden, gate_values, up_values):
        grad_hidden = grad_hidden.astype(F32)
        gate_values, up_values = gate_values.astype(F32), up_values.astype(F32)
        sigmoid = jax.nn.sigmoid(gate_values)
        activated = gate_values * sigmoid
        hidden = (activated * up_values).astype(BF16)
        grad_gate = (grad_hidden * up_values * sigmoid * (1.0 + gate_values * (1.0 - sigmoid))).astype(BF16)
        grad_up = (grad_hidden * activated).astype(BF16)
        return hidden, grad_gate, grad_up

    gate_near, gate_other = halves(gate_all)
    up_near, up_other = halves(up_all)
    hidden_other = spread(grad_hidden[share // 2 :])
    hidden_near = spread(grad_hidden[: share // 2])
    other = back(hidden_other, gate_other, up_other)
    near = back(hidden_near, gate_near, up_near)

    def in_part(half):
        value = against_weight(half[1], gate_pair) + against_weight(half[2], up_pair)
        return value.reshape(chips, ring, rows, wide)

    outward = in_part(other).astype(BF16)
    inward = in_part(near)
    total = None
    for group in ((4, 3, 5), (2, 6, 1, 7, 0)):
        come = swap(jnp.stack([outward[:, k] for k in group], axis=0), "xl")
        for i, k in enumerate(group):
            block = inward[:, k] + come[i].astype(F32)
            if k == 4:
                block = block.astype(BF16)
                half = chips // 2
                block = jnp.concatenate([shift(block[:half], "z", 4), shift(block[half:], "z", -4)], axis=0).astype(F32)
            elif k > 0:
                block = shift(block.astype(BF16), "z", k if k < 4 else k - ring).astype(F32)
            total = block if total is None else total + block
    summed = total.astype(BF16)
    mine, theirs = summed[:, :, :narrow], swap(summed[:, :, narrow:], "c")
    first, second = jnp.where(core == 0, mine, theirs), jnp.where(core == 0, theirs, mine)
    input_grad = jnp.stack([first, second], axis=1).reshape(2 * chips, rows, narrow)

    def whole(i):
        parts = [value[i].reshape(chips, share // 2, units) for value in (near, other)]
        return jnp.concatenate(parts, axis=1).reshape(tokens, units)

    hidden, grad_gate, grad_up = whole(0), whole(1), whole(2)
    down_grad = contract_rows(hidden, grad_cols[:, :narrow]) + swap(
        contract_rows(hidden, grad_cols[:, narrow:]), "c"
    )
    gate_grad = contract_rows(in_cols[:, :narrow], grad_gate) + swap(
        contract_rows(in_cols[:, narrow:], grad_gate), "c"
    )
    up_grad = contract_rows(in_cols[:, :narrow], grad_up) + swap(
        contract_rows(in_cols[:, narrow:], grad_up), "c"
    )
    return (input_grad, gate_grad, up_grad, down_grad)


def solution(mesh):
    grid = Mesh(mesh.devices.reshape(2, 4, 2, 2, 8), ("xh", "y", "c", "xl", "z"))
    dp, tensor = ("xh", "y", "c"), ("xl", "z")
    in_specs = (
        P(dp + tensor, None),
        P(dp + tensor, None),
        P(dp, tensor),
        P(dp, tensor),
        P(dp, tensor),
        P(dp, tensor),
        P(tensor, dp),
    )
    out_specs = (P(None, tensor, dp), P(dp, tensor), P(dp, tensor), P(tensor, dp))
    return jax.shard_map(shards, mesh=grid, in_specs=in_specs, out_specs=out_specs, check_vma=False)
```

```python
import jax
import jax.numpy as jnp
from jax import lax
from jax.experimental import pallas as pl
from jax.experimental.pallas import tpu as pltpu
from jax.sharding import Mesh, PartitionSpec as P

BF16 = jnp.bfloat16
F32 = jnp.float32
CHIPS = ("xh", "y")
PLANE = ("xh", "y", "xl")


def swap(value, axis):
    return lax.ppermute(value, axis, [(0, 1), (1, 0)])


def shift(value, axis, by):
    size = lax.axis_size(axis)
    return lax.ppermute(value, axis, [(i, (i + by) % size) for i in range(size)])


def after(value, *others):
    return lax.optimization_barrier((value, *others))[0]


def ring_gather(own):
    z = lax.axis_index("z")
    chips, rows, wide = own.shape
    half = chips // 2
    whole = jnp.zeros((chips, 8, rows, wide), own.dtype)

    def put(whole, block, by, first=0):
        place = lax.rem(z + by + 8, 8)
        return lax.dynamic_update_slice(whole, block[:, None], (first, place, 0, 0))

    whole = put(whole, own, 0)
    right = left = own
    for by in range(1, 4):
        right, left = shift(right, "z", 1), shift(left, "z", -1)
        whole = put(put(whole, right, -by), left, by)
    right, left = shift(right[:half], "z", 1), shift(left[half:], "z", -1)
    return put(put(whole, right, 4), left, 4, half), (right, left)


def ring_scatter(blocks):
    z = lax.axis_index("z")
    half = blocks.shape[0] // 2

    def block(k):
        return lax.dynamic_index_in_dim(blocks, lax.rem(z + k, 8), axis=2, keepdims=False)

    far = block(4).astype(BF16)
    right, left = shift(far[:half], "z", 1), shift(far[half:], "z", -1)
    for k in (3, 2, 1):
        mine, other = block(k), block(8 - k)
        if k == 3:
            mine = jnp.concatenate([mine[:half] + right.astype(F32), mine[half:]], axis=0)
            other = jnp.concatenate([other[:half], other[half:] + left.astype(F32)], axis=0)
        else:
            mine = mine + right.astype(F32)
            other = other + left.astype(F32)
        if k > 1:
            mine, other = mine.astype(BF16), other.astype(BF16)
        right, left = shift(mine, "z", 1), shift(other, "z", -1)
    return block(0) + right + left


def contract_rows(left, right):
    return lax.dot_general(left, right, (((0,), (0,)), ((), ())), preferred_element_type=F32)


def against_weight(left, weight):
    return lax.dot_general(left, weight, (((1,), (1,)), ((), ())), preferred_element_type=F32)


def part_kernel(place, grad, near_own, near_other, far_own, far_other, out):
    narrow = near_own.shape[1]
    shape = out.shape[0], out.shape[2], out.shape[3]
    for flip, (own, other) in enumerate(((near_own, near_other), (far_own, far_other))):
        value = against_weight(grad[:, :narrow], own[...]) + against_weight(grad[:, narrow:], other[...])
        out[:, place[0] ^ flip] = value.astype(BF16).reshape(shape)


def partial_product(x_lo, grad, weights, chips):
    tokens, units = grad.shape[0], weights[0].shape[0]
    vmem = pl.BlockSpec(memory_space=pltpu.VMEM)
    return pl.pallas_call(
        part_kernel,
        out_shape=jax.ShapeDtypeStruct((chips, 2, tokens // chips, units), BF16),
        in_specs=[pl.BlockSpec(memory_space=pltpu.SMEM)] + [vmem] * 5,
        out_specs=vmem,
        compiler_params=pltpu.CompilerParams(vmem_limit_bytes=40 * 2**20),
        cost_estimate=pl.CostEstimate(flops=4 * tokens * units * grad.shape[1], bytes_accessed=7 * 2**20, transcendentals=0),
    )(x_lo.reshape(1), grad, *weights)


def shards(inputs, out_grad, gate_pre, up_pre, gate_weight, up_weight, down_weight):
    core, x_lo = lax.axis_index("c"), lax.axis_index("xl")
    rows = inputs.shape[0]
    chips = lax.axis_size(CHIPS)
    ring = lax.axis_size("z")
    wide = inputs.shape[1] // chips
    narrow = wide // 2
    share, units = gate_pre.shape
    tokens = chips * share

    def by_chip(value):
        return value.reshape(rows, chips, wide).transpose(1, 0, 2)

    gate_all = lax.all_gather(gate_pre, CHIPS, axis=0, tiled=True)

    both = jnp.concatenate([by_chip(out_grad), by_chip(inputs)], axis=1)
    both = lax.all_to_all(both, CHIPS, split_axis=0, concat_axis=0, tiled=True)
    both = jnp.where(core == 0, both, jnp.roll(both, narrow, axis=2))
    own_grad, own_in = both[:, :rows], both[:, rows:]

    down_far = swap(down_weight, "xl")
    down_pieces = (down_weight, swap(down_weight, "c"), down_far, swap(down_far, "c"))
    gate_pair = jnp.concatenate([gate_weight, swap(gate_weight, "c")], axis=0)
    up_pair = jnp.concatenate([up_weight, swap(up_weight, "c")], axis=0)

    def spread(value):
        value = jnp.broadcast_to(value[None], (chips, *value.shape))
        value = lax.all_to_all(value, CHIPS, split_axis=0, concat_axis=0, tiled=True)
        return value.reshape(tokens, units)

    up_all = spread(after(up_pre, both))

    near_cols, last = ring_gather(own_grad)
    part = partial_product(x_lo, near_cols.reshape(tokens // 2, wide), down_pieces, chips)
    part = part.reshape(2 * chips, share // 2, units)
    part = lax.all_to_all(part, PLANE, split_axis=0, concat_axis=0, tiled=True)
    part = part.reshape(chips, share, units)
    grad_hidden = spread(jnp.sum(part.astype(F32), axis=0).astype(BF16))

    in_cols = lax.all_gather(after(own_in, gate_all), ("xl", "z"), axis=0, tiled=False)
    in_cols = in_cols.transpose(1, 0, 2, 3).reshape(tokens, wide)

    gate_values, up_values = gate_all.astype(F32), up_all.astype(F32)
    hidden = (gate_values * jax.nn.sigmoid(gate_values) * up_values).astype(BF16)
    grad_hidden, hidden = lax.optimization_barrier((grad_hidden, hidden))
    grad_hidden = grad_hidden.astype(F32)
    sigmoid = jax.nn.sigmoid(gate_values)
    grad_gate = (grad_hidden * up_values * sigmoid * (1.0 + gate_values * (1.0 - sigmoid))).astype(BF16)
    grad_up = (grad_hidden * gate_values * sigmoid).astype(BF16)

    in_part = against_weight(grad_gate, gate_pair) + against_weight(grad_up, up_pair)
    summed = ring_scatter(in_part.reshape(chips, 2, ring, rows, wide))
    mine, theirs = (
        lax.dynamic_index_in_dim(summed, place, axis=1, keepdims=False) for place in (x_lo, 1 - x_lo)
    )
    summed = (mine + swap(theirs, "xl")).astype(BF16)
    mine, theirs = summed[:, :, :narrow], swap(summed[:, :, narrow:], "c")
    first, second = jnp.where(core == 0, mine, theirs), jnp.where(core == 0, theirs, mine)
    input_grad = jnp.stack([first, second], axis=1).reshape(2 * chips, rows, narrow)

    def both_cores(mine, theirs):
        return mine() + swap(theirs().astype(BF16), "c").astype(F32)

    near_cols, grad_hidden = lax.optimization_barrier((near_cols, grad_hidden))
    far_cols = swap(near_cols, "xl")
    cols = jnp.where(x_lo == 0, jnp.stack([near_cols, far_cols], 1), jnp.stack([far_cols, near_cols], 1))
    cols = cols.reshape(tokens, wide)
    gate_grad = both_cores(
        lambda: contract_rows(in_cols[:, :narrow], grad_gate),
        lambda: contract_rows(in_cols[:, narrow:], grad_gate),
    )
    up_grad = both_cores(
        lambda: contract_rows(in_cols[:, :narrow], grad_up),
        lambda: contract_rows(in_cols[:, narrow:], grad_up),
    )
    down_grad = both_cores(
        lambda: contract_rows(hidden, cols[:, :narrow]),
        lambda: contract_rows(hidden, cols[:, narrow:]),
    )
    return (input_grad, gate_grad, up_grad, down_grad)


def solution(mesh):
    grid = Mesh(mesh.devices.reshape(2, 4, 2, 2, 8), ("xh", "y", "c", "xl", "z"))
    dp, tensor = ("xh", "y", "c"), ("xl", "z")
    in_specs = (
        P(dp + tensor, None),
        P(dp + tensor, None),
        P(dp, tensor),
        P(dp, tensor),
        P(dp, tensor),
        P(dp, tensor),
        P(tensor, dp),
    )
    out_specs = (P(None, tensor, dp), P(dp, tensor), P(dp, tensor), P(tensor, dp))
    return jax.shard_map(shards, mesh=grid, in_specs=in_specs, out_specs=out_specs, check_vma=False)
```

```python
import jax
import jax.numpy as jnp
from jax import lax
from jax.experimental import pallas as pl
from jax.experimental.pallas import tpu as pltpu
from jax.sharding import Mesh, PartitionSpec as P

BF16 = jnp.bfloat16
F32 = jnp.float32
CHIPS = ("xh", "y")
PLANE = ("xh", "y", "xl")


def swap(value, axis):
    return lax.ppermute(value, axis, [(0, 1), (1, 0)])


def shift(value, axis, by):
    size = lax.axis_size(axis)
    return lax.ppermute(value, axis, [(i, (i + by) % size) for i in range(size)])


def after(value, *others):
    return lax.optimization_barrier((value, *others))[0]


def ring_gather(own):
    z = lax.axis_index("z")
    chips, rows, wide = own.shape
    half = chips // 2
    whole = jnp.zeros((chips, 8, rows, wide), own.dtype)

    def put(whole, block, by, first=0):
        place = lax.rem(z + by + 8, 8)
        return lax.dynamic_update_slice(whole, block[:, None], (first, place, 0, 0))

    whole = put(whole, own, 0)
    right = left = own
    for by in range(1, 4):
        right, left = shift(right, "z", 1), shift(left, "z", -1)
        whole = put(put(whole, right, -by), left, by)
    right, left = shift(right[:half], "z", 1), shift(left[half:], "z", -1)
    return put(put(whole, right, 4), left, 4, half)


def ring_scatter(blocks):
    z = lax.axis_index("z")
    half = blocks.shape[0] // 2

    def block(k):
        return lax.dynamic_index_in_dim(blocks, lax.rem(z + k, 8), axis=2, keepdims=False)

    far = block(4).astype(BF16)
    right, left = shift(far[:half], "z", 1), shift(far[half:], "z", -1)
    for k in (3, 2, 1):
        mine, other = block(k), block(8 - k)
        if k == 3:
            mine = jnp.concatenate([mine[:half] + right.astype(F32), mine[half:]], axis=0)
            other = jnp.concatenate([other[:half], other[half:] + left.astype(F32)], axis=0)
        else:
            mine = mine + right.astype(F32)
            other = other + left.astype(F32)
        if k > 1:
            mine, other = mine.astype(BF16), other.astype(BF16)
        right, left = shift(mine, "z", 1), shift(other, "z", -1)
    return block(0) + right + left


def back_kernel(grad, gate, up, gate_own, gate_other, up_own, up_other, grad_gate, grad_up, out):
    narrow = gate_own.shape[0]
    gate_values, up_values = gate[...].astype(F32), up[...].astype(F32)
    grad_hidden = grad[...].astype(F32)
    sigmoid = jax.nn.sigmoid(gate_values)
    slope = sigmoid * (1.0 + gate_values * (1.0 - sigmoid))
    grad_gate[...] = (grad_hidden * up_values * slope).astype(BF16)
    grad_up[...] = (grad_hidden * (gate_values * sigmoid)).astype(BF16)
    left, right = grad_gate[...], grad_up[...]
    out[:, :narrow] = against_weight(left, gate_own[...]) + against_weight(right, up_own[...])
    out[:, narrow:] = against_weight(left, gate_other[...]) + against_weight(right, up_other[...])


def swiglu_back(grad, gate, up, weights, wide):
    tokens, units = grad.shape
    step = min(256, tokens)
    moving = pl.BlockSpec((step, units), lambda i: (i, 0))
    fixed = pl.BlockSpec(weights[0].shape, lambda i: (0, 0))
    return pl.pallas_call(
        back_kernel,
        grid=(tokens // step,),
        out_shape=(
            jax.ShapeDtypeStruct((tokens, units), BF16),
            jax.ShapeDtypeStruct((tokens, units), BF16),
            jax.ShapeDtypeStruct((tokens, wide), F32),
        ),
        in_specs=[moving] * 3 + [fixed] * 4,
        out_specs=(moving, moving, pl.BlockSpec((step, wide), lambda i: (i, 0))),
        compiler_params=pltpu.CompilerParams(vmem_limit_bytes=40 * 2**20),
        cost_estimate=pl.CostEstimate(
            flops=4 * tokens * units * wide, bytes_accessed=18 * 2**20, transcendentals=tokens * units
        ),
    )(grad, gate, up, *weights)


def contract_rows(left, right):
    return lax.dot_general(left, right, (((0,), (0,)), ((), ())), preferred_element_type=F32)


def against_weight(left, weight):
    return lax.dot_general(left, weight, (((1,), (1,)), ((), ())), preferred_element_type=F32)


def part_kernel(place, grad, near_own, near_other, far_own, far_other, out):
    narrow = near_own.shape[1]
    shape = out.shape[0], out.shape[2], out.shape[3]
    for flip, (own, other) in enumerate(((near_own, near_other), (far_own, far_other))):
        value = against_weight(grad[:, :narrow], own[...]) + against_weight(grad[:, narrow:], other[...])
        out[:, place[0] ^ flip] = value.astype(BF16).reshape(shape)


def partial_product(x_lo, grad, weights, chips):
    tokens, units = grad.shape[0], weights[0].shape[0]
    vmem = pl.BlockSpec(memory_space=pltpu.VMEM)
    return pl.pallas_call(
        part_kernel,
        out_shape=jax.ShapeDtypeStruct((chips, 2, tokens // chips, units), BF16),
        in_specs=[pl.BlockSpec(memory_space=pltpu.SMEM)] + [vmem] * 5,
        out_specs=vmem,
        compiler_params=pltpu.CompilerParams(vmem_limit_bytes=40 * 2**20),
        cost_estimate=pl.CostEstimate(flops=4 * tokens * units * grad.shape[1], bytes_accessed=7 * 2**20, transcendentals=0),
    )(x_lo.reshape(1), grad, *weights)


def shards(inputs, out_grad, gate_pre, up_pre, gate_weight, up_weight, down_weight):
    core, x_lo = lax.axis_index("c"), lax.axis_index("xl")
    rows = inputs.shape[0]
    chips = lax.axis_size(CHIPS)
    ring = lax.axis_size("z")
    wide = inputs.shape[1] // chips
    narrow = wide // 2
    share, units = gate_pre.shape
    tokens = chips * share

    def by_chip(value):
        return value.reshape(rows, chips, wide).transpose(1, 0, 2)

    gate_all = lax.all_gather(gate_pre, CHIPS, axis=0, tiled=True)

    both = jnp.concatenate([by_chip(out_grad), by_chip(inputs)], axis=1)
    both = lax.all_to_all(both, CHIPS, split_axis=0, concat_axis=0, tiled=True)
    both = jnp.where(core == 0, both, jnp.roll(both, narrow, axis=2))
    both_far = swap(both, "xl")

    down_far = swap(down_weight, "xl")
    down_pieces = (down_weight, swap(down_weight, "c"), down_far, swap(down_far, "c"))
    back_pieces = (gate_weight, swap(gate_weight, "c"), up_weight, swap(up_weight, "c"))

    def spread(value):
        value = jnp.broadcast_to(value[None], (chips, *value.shape))
        value = lax.all_to_all(value, CHIPS, split_axis=0, concat_axis=0, tiled=True)
        return value.reshape(tokens, units)

    up_all = spread(after(up_pre, both))

    near_grad = ring_gather(both[:, :rows])
    part = partial_product(x_lo, near_grad.reshape(tokens // 2, wide), down_pieces, chips)
    part, up_all, *back_pieces = lax.optimization_barrier((part, up_all, *back_pieces))
    second = jnp.concatenate([both_far[:, :rows], both[:, rows:]], axis=1)
    second, near_grad = lax.optimization_barrier((second, near_grad))
    part = part.reshape(2 * chips, share // 2, units)
    part = lax.all_to_all(part, PLANE, split_axis=0, concat_axis=0, tiled=True)
    part = part.reshape(chips, share, units)
    grad_hidden = jnp.sum(part.astype(F32), axis=0).astype(BF16)

    second = ring_gather(second)
    grad_hidden, second, gate_all = lax.optimization_barrier((grad_hidden, second, gate_all))
    far_grad, near_in = second[:, :, :rows], second[:, :, rows:]
    grad_hidden = spread(grad_hidden)
    far_in = ring_gather(after(both_far[:, rows:], second))

    def join(near, far):
        pair = jnp.where(x_lo == 0, jnp.stack([near, far], 1), jnp.stack([far, near], 1))
        return pair.reshape(tokens, wide)

    gate_values, up_values = gate_all.astype(F32), up_all.astype(F32)
    hidden = (gate_values * jax.nn.sigmoid(gate_values) * up_values).astype(BF16)
    grad_cols = join(near_grad, far_grad)
    grad_hidden, hidden, far_in, grad_cols = lax.optimization_barrier((grad_hidden, hidden, far_in, grad_cols))
    in_cols = join(near_in, far_in)

    grad_gate, grad_up, in_part = swiglu_back(grad_hidden, gate_all, up_all, back_pieces, wide)
    summed = ring_scatter(in_part.reshape(chips, 2, ring, rows, wide))
    mine, theirs = (
        lax.dynamic_index_in_dim(summed, place, axis=1, keepdims=False) for place in (x_lo, 1 - x_lo)
    )
    summed = (mine + swap(theirs, "xl")).astype(BF16)
    mine, theirs = summed[:, :, :narrow], swap(summed[:, :, narrow:], "c")
    first, second = jnp.where(core == 0, mine, theirs), jnp.where(core == 0, theirs, mine)
    input_grad = jnp.stack([first, second], axis=1).reshape(2 * chips, rows, narrow)

    def both_cores(mine, theirs):
        return mine() + swap(theirs().astype(BF16), "c").astype(F32)

    gate_grad = both_cores(
        lambda: contract_rows(in_cols[:, :narrow], grad_gate),
        lambda: contract_rows(in_cols[:, narrow:], grad_gate),
    )
    up_grad = both_cores(
        lambda: contract_rows(in_cols[:, :narrow], grad_up),
        lambda: contract_rows(in_cols[:, narrow:], grad_up),
    )
    down_grad = both_cores(
        lambda: contract_rows(hidden, grad_cols[:, :narrow]),
        lambda: contract_rows(hidden, grad_cols[:, narrow:]),
    )
    return (input_grad, gate_grad, up_grad, down_grad)


def solution(mesh):
    grid = Mesh(mesh.devices.reshape(2, 4, 2, 2, 8), ("xh", "y", "c", "xl", "z"))
    dp, tensor = ("xh", "y", "c"), ("xl", "z")
    in_specs = (
        P(dp + tensor, None),
        P(dp + tensor, None),
        P(dp, tensor),
        P(dp, tensor),
        P(dp, tensor),
        P(dp, tensor),
        P(tensor, dp),
    )
    out_specs = (P(None, tensor, dp), P(dp, tensor), P(dp, tensor), P(tensor, dp))
    return jax.shard_map(shards, mesh=grid, in_specs=in_specs, out_specs=out_specs, check_vma=False)
```

```python
import jax
import jax.numpy as jnp
from jax import lax
from jax.experimental import pallas as pl
from jax.experimental.pallas import tpu as pltpu
from jax.sharding import Mesh, PartitionSpec as P

BF16 = jnp.bfloat16
F32 = jnp.float32
CHIPS = ("xh", "y")
PLANE = ("xh", "y", "xl")


def swap(value, axis):
    return lax.ppermute(value, axis, [(0, 1), (1, 0)])


def shift(value, axis, by):
    size = lax.axis_size(axis)
    return lax.ppermute(value, axis, [(i, (i + by) % size) for i in range(size)])


def after(value, *others):
    return lax.optimization_barrier((value, *others))[0]


def ring_gather(own):
    z = lax.axis_index("z")
    chips, rows, wide = own.shape
    half = chips // 2
    whole = jnp.zeros((chips, 8, rows, wide), own.dtype)

    def put(whole, block, by, first=0):
        place = lax.rem(z + by + 8, 8)
        return lax.dynamic_update_slice(whole, block[:, None], (first, place, 0, 0))

    whole = put(whole, own, 0)
    right = left = own
    landed = []
    for by in range(1, 4):
        right, left = shift(right, "z", 1), shift(left, "z", -1)
        whole = put(put(whole, right, -by), left, by)
        landed.append((right, left))

    def last(*hold):
        (right, left), _ = lax.optimization_barrier((landed[-1], hold))
        right, left = shift(right[:half], "z", 1), shift(left[half:], "z", -1)
        return put(put(whole, right, 4), left, 4, half)

    return last, landed


def beside(send, job, *given):
    send, given = lax.optimization_barrier((send, given))
    landed = (shift(send[0], "z", 1), shift(send[1], "z", -1))
    return lax.optimization_barrier((landed, job(*given)))


def ring_scatter(blocks, jobs, given):
    z = lax.axis_index("z")
    half = blocks.shape[0] // 2

    def block(k):
        return lax.dynamic_index_in_dim(blocks, lax.rem(z + k, 8), axis=2, keepdims=False)

    far = block(4).astype(BF16)
    (right, left), state = beside((far[:half], far[half:]), jobs[0], *given)
    for k, job in zip((3, 2, 1), jobs[1:]):
        mine, other = block(k), block(8 - k)
        if k == 3:
            mine = jnp.concatenate([mine[:half] + right.astype(F32), mine[half:]], axis=0)
            other = jnp.concatenate([other[:half], other[half:] + left.astype(F32)], axis=0)
        else:
            mine = mine + right.astype(F32)
            other = other + left.astype(F32)
        if k > 1:
            mine, other = mine.astype(BF16), other.astype(BF16)
        (right, left), state = beside((mine, other), job, *state)
    return block(0) + right + left, state


def sum_kernel(parts, out):
    total = jnp.sum(parts[...].astype(F32), axis=0).astype(BF16)
    for i in range(out.shape[0]):
        out[i] = total


def sum_and_copy(parts):
    count, rows, units = parts.shape
    step = rows // 4
    spec = pl.BlockSpec((count, step, units), lambda i: (0, i, 0))
    return pl.pallas_call(
        sum_kernel,
        grid=(4,),
        out_shape=jax.ShapeDtypeStruct(parts.shape, BF16),
        in_specs=[spec],
        out_specs=spec,
        compiler_params=pltpu.CompilerParams(vmem_limit_bytes=56 * 2**20),
        cost_estimate=pl.CostEstimate(flops=parts.size, bytes_accessed=4 * parts.size, transcendentals=0),
    )(parts)


def back_kernel(grad, gate_slope, up_slope, gate_own, gate_other, up_own, up_other, grad_gate, grad_up, out):
    narrow = gate_own.shape[0]
    grad_hidden = grad[...].astype(F32)
    left = (grad_hidden * gate_slope[...]).astype(BF16)
    right = (grad_hidden * up_slope[...]).astype(BF16)
    grad_gate[...], grad_up[...] = left, right
    out[:, :narrow] = against_weight(left, gate_own[...]) + against_weight(right, up_own[...])
    out[:, narrow:] = against_weight(left, gate_other[...]) + against_weight(right, up_other[...])


def swiglu_back(grad, gate_slope, up_slope, weights, wide):
    tokens, units = grad.shape
    step = min(256, tokens)
    moving = pl.BlockSpec((step, units), lambda i: (i, 0))
    fixed = pl.BlockSpec(weights[0].shape, lambda i: (0, 0))
    return pl.pallas_call(
        back_kernel,
        grid=(tokens // step,),
        out_shape=(
            jax.ShapeDtypeStruct((tokens, units), BF16),
            jax.ShapeDtypeStruct((tokens, units), BF16),
            jax.ShapeDtypeStruct((tokens, wide), F32),
        ),
        in_specs=[moving] * 3 + [fixed] * 4,
        out_specs=(moving, moving, pl.BlockSpec((step, wide), lambda i: (i, 0))),
        compiler_params=pltpu.CompilerParams(vmem_limit_bytes=56 * 2**20),
        cost_estimate=pl.CostEstimate(flops=4 * tokens * units * wide, bytes_accessed=22 * 2**20, transcendentals=0),
    )(grad, gate_slope, up_slope, *weights)


def contract_rows(left, right):
    return lax.dot_general(left, right, (((0,), (0,)), ((), ())), preferred_element_type=F32)


def against_weight(left, weight):
    return lax.dot_general(left, weight, (((1,), (1,)), ((), ())), preferred_element_type=F32)


def part_kernel(place, grad, near_own, near_other, far_own, far_other, out):
    narrow = near_own.shape[1]
    shape = out.shape[0], out.shape[2], out.shape[3]
    for flip, (own, other) in enumerate(((near_own, near_other), (far_own, far_other))):
        value = against_weight(grad[:, :narrow], own[...]) + against_weight(grad[:, narrow:], other[...])
        out[:, place[0] ^ flip] = value.astype(BF16).reshape(shape)


def partial_product(x_lo, grad, weights, chips):
    tokens, units = grad.shape[0], weights[0].shape[0]
    vmem = pl.BlockSpec(memory_space=pltpu.VMEM)
    return pl.pallas_call(
        part_kernel,
        out_shape=jax.ShapeDtypeStruct((chips, 2, tokens // chips, units), BF16),
        in_specs=[pl.BlockSpec(memory_space=pltpu.SMEM)] + [vmem] * 5,
        out_specs=vmem,
        compiler_params=pltpu.CompilerParams(vmem_limit_bytes=56 * 2**20),
        cost_estimate=pl.CostEstimate(flops=4 * tokens * units * grad.shape[1], bytes_accessed=7 * 2**20, transcendentals=0),
    )(x_lo.reshape(1), grad, *weights)


def shards(inputs, out_grad, gate_pre, up_pre, gate_weight, up_weight, down_weight):
    core, x_lo = lax.axis_index("c"), lax.axis_index("xl")
    rows = inputs.shape[0]
    chips = lax.axis_size(CHIPS)
    ring = lax.axis_size("z")
    wide = inputs.shape[1] // chips
    narrow = wide // 2
    share, units = gate_pre.shape
    tokens = chips * share

    def by_chip(value):
        return value.reshape(rows, chips, wide).transpose(1, 0, 2)

    gate_all = lax.all_gather(gate_pre, CHIPS, axis=0, tiled=True)

    both = jnp.concatenate([by_chip(out_grad), by_chip(inputs)], axis=1)
    both = lax.all_to_all(both, CHIPS, split_axis=0, concat_axis=0, tiled=True)
    both = jnp.where(core == 0, both, jnp.roll(both, narrow, axis=2))
    both_far = swap(both, "xl")

    down_far = swap(down_weight, "xl")
    down_pieces = (down_weight, swap(down_weight, "c"), down_far, swap(down_far, "c"))
    back_pieces = (gate_weight, swap(gate_weight, "c"), up_weight, swap(up_weight, "c"))

    def spread(value):
        value = jnp.broadcast_to(value[None], (chips, *value.shape))
        value = lax.all_to_all(value, CHIPS, split_axis=0, concat_axis=0, tiled=True)
        return value.reshape(tokens, units)

    up_all = spread(after(up_pre, both))

    near_grad = ring_gather(both[:, :rows])[0]()
    part = partial_product(x_lo, near_grad.reshape(tokens // 2, wide), down_pieces, chips)
    part, up_all, *back_pieces = lax.optimization_barrier((part, up_all, *back_pieces))
    sent = part = part.reshape(2 * chips, share // 2, units)
    part = lax.all_to_all(part, PLANE, split_axis=0, concat_axis=0, tiled=True)

    second = jnp.concatenate([after(both_far, sent), both[:, rows:]], axis=1)
    last, landed = ring_gather(second)
    part, landed[1] = lax.optimization_barrier((part, landed[1]))
    grad_hidden = sum_and_copy(part.reshape(chips, share, units))
    grad_hidden, gate_all = lax.optimization_barrier((grad_hidden, gate_all))
    second = last(grad_hidden)
    grad_hidden = lax.all_to_all(grad_hidden, CHIPS, split_axis=0, concat_axis=0, tiled=True)
    grad_hidden = grad_hidden.reshape(tokens, units)

    def join(near, far):
        pair = jnp.where(x_lo == 0, jnp.stack([near, far], 1), jnp.stack([far, near], 1))
        return pair.reshape(tokens, wide)

    grad_cols = join(near_grad, second[:, :, :rows])
    in_cols = join(second[:, :, 2 * rows :], second[:, :, rows : 2 * rows])
    gate_values, up_values = gate_all.astype(F32), up_all.astype(F32)
    sigmoid = jax.nn.sigmoid(gate_values)
    up_slope = gate_values * sigmoid
    gate_slope = up_values * sigmoid * (1.0 + gate_values * (1.0 - sigmoid))
    hidden = (up_slope * up_values).astype(BF16)

    def finish(left, right, landed):
        return contract_rows(left, right) + landed.astype(F32)

    down_grad = finish(
        hidden, grad_cols[:, :narrow], swap(contract_rows(hidden, grad_cols[:, narrow:]).astype(BF16), "c")
    )
    grad_hidden, gate_slope, up_slope, in_cols, down_grad = lax.optimization_barrier(
        (grad_hidden, gate_slope, up_slope, in_cols, down_grad)
    )
    grad_gate, grad_up, in_part = swiglu_back(grad_hidden, gate_slope, up_slope, back_pieces, wide)

    def others(*values):
        return tuple(contract_rows(in_cols[:, narrow:], value).astype(BF16) for value in values)

    jobs = (
        lambda *values: values,
        others,
        lambda gate, up: (swap(gate, "c"), swap(up, "c")),
        lambda gate, up: (finish(in_cols[:, :narrow], grad_gate, gate), up),
    )
    summed, (gate_grad, up_grad) = ring_scatter(in_part.reshape(chips, 2, ring, rows, wide), jobs, (grad_gate, grad_up))
    up_grad = finish(in_cols[:, :narrow], grad_up, up_grad)
    mine, theirs = (
        lax.dynamic_index_in_dim(summed, place, axis=1, keepdims=False) for place in (x_lo, 1 - x_lo)
    )
    summed = (mine + swap(theirs, "xl")).astype(BF16)
    mine, theirs = summed[:, :, :narrow], swap(summed[:, :, narrow:], "c")
    first, second = jnp.where(core == 0, mine, theirs), jnp.where(core == 0, theirs, mine)
    input_grad = jnp.stack([first, second], axis=1).reshape(2 * chips, rows, narrow)
    return (input_grad, gate_grad, up_grad, down_grad)


def solution(mesh):
    grid = Mesh(mesh.devices.reshape(2, 4, 2, 2, 8), ("xh", "y", "c", "xl", "z"))
    dp, tensor = ("xh", "y", "c"), ("xl", "z")
    in_specs = (
        P(dp + tensor, None),
        P(dp + tensor, None),
        P(dp, tensor),
        P(dp, tensor),
        P(dp, tensor),
        P(dp, tensor),
        P(tensor, dp),
    )
    out_specs = (P(None, tensor, dp), P(dp, tensor), P(dp, tensor), P(tensor, dp))
    return jax.shard_map(shards, mesh=grid, in_specs=in_specs, out_specs=out_specs, check_vma=False)
```

```python
import functools

import jax
import jax.numpy as jnp
from jax import lax
from jax.experimental import pallas as pl
from jax.experimental.pallas import tpu as pltpu
from jax.sharding import Mesh, PartitionSpec as P

BF16 = jnp.bfloat16
F32 = jnp.float32
CHIPS = ("xh", "y")
PLANE = ("xh", "y", "xl")


def swap(value, axis):
    return lax.ppermute(value, axis, [(0, 1), (1, 0)])


def shift(value, axis, by):
    size = lax.axis_size(axis)
    return lax.ppermute(value, axis, [(i, (i + by) % size) for i in range(size)])


def ring_gather(own):
    z = lax.axis_index("z")
    chips, rows, wide = own.shape
    half = chips // 2
    whole = jnp.zeros((chips, 8, rows, wide), own.dtype)

    def put(whole, block, by, first=0):
        place = lax.rem(z + by + 8, 8)
        return lax.dynamic_update_slice(whole, block[:, None], (first, place, 0, 0))

    whole = put(whole, own, 0)
    right = left = own
    landed = []
    for by in range(1, 4):
        right, left = shift(right, "z", 1), shift(left, "z", -1)
        whole = put(put(whole, right, -by), left, by)
        landed.append((right, left))

    def last(hold=()):
        (right, left), hold = lax.optimization_barrier((landed[-1], hold))
        right, left = shift(right[:half], "z", 1), shift(left[half:], "z", -1)
        return put(put(whole, right, 4), left, 4, half), hold

    return last, landed


def sum_kernel(place, parts, out):
    total = jnp.sum(parts[...].astype(F32), axis=0).astype(BF16)
    for i in range(out.shape[0]):
        out[i] = total


def sum_and_copy(parts, place):
    count, _, rows, units = parts.shape
    step = rows // 2
    return pl.pallas_call(
        sum_kernel,
        grid_spec=pltpu.PrefetchScalarGridSpec(
            num_scalar_prefetch=1,
            grid=(2,),
            in_specs=[pl.BlockSpec((count, None, step, units), lambda i, place: (0, place[0], i, 0))],
            out_specs=pl.BlockSpec((count, step, units), lambda i, place: (0, i, 0)),
        ),
        out_shape=jax.ShapeDtypeStruct((count, rows, units), BF16),
        compiler_params=pltpu.CompilerParams(vmem_limit_bytes=24 * 2**20),
        cost_estimate=pl.CostEstimate(flops=parts.size, bytes_accessed=2 * parts.size, transcendentals=0),
    )(place.reshape(1), parts)


def back_kernel(place, grad, gate, up, gate_own, gate_other, up_own, up_other, *refs, spread):
    grad_gate, grad_up = refs[-3 - spread : -1 - spread]
    outs, product = refs[-1 - spread : -1], refs[-1]
    narrow = gate_own.shape[0]
    chips, share, units = grad.shape
    _, ring, rows, _ = product.shape
    gate_values, up_values = gate[...].astype(F32), up[...].astype(F32)
    grad_hidden = grad[...].astype(F32)
    sigmoid = jax.nn.sigmoid(gate_values)
    slope = sigmoid * (1.0 + gate_values * (1.0 - sigmoid))
    left = (grad_hidden * up_values * slope).astype(BF16)
    right = (grad_hidden * (gate_values * sigmoid)).astype(BF16)
    grad_gate[...], grad_up[...] = left, right
    left, right = left.reshape(chips * share, units), right.reshape(chips * share, units)
    pieces = ((gate_own, up_own), (gate_other, up_other))
    for i, (first, second) in enumerate(pieces):
        value = against_weight(left, first[...]) + against_weight(right, second[...])
        product[:, :, :, i * narrow : (i + 1) * narrow] = value.reshape(chips, ring, rows, narrow)
    for k in range(ring):
        if spread > 1:
            outs[k][...] = product[:, lax.rem(place[1] + k, ring)].astype(BF16)
        else:
            outs[0][k] = product[:, k].astype(BF16)


def swiglu_back(place, half, grad, gate, up, weights, before, wide, rows, spread):
    chips, share, units = grad.shape
    ring = share // rows
    step = chips // 2
    count = ring if spread else 1
    chunk = pl.BlockSpec((step, share, units), lambda i, place: (i, 0, 0))
    stash = pl.BlockSpec((step, None, share, units), lambda i, place: (i, place[0], 0, 0))
    fixed = pl.BlockSpec(weights[0].shape, lambda i, place: (0, 0))
    wanted = pl.BlockSpec((None, step, share, units), lambda i, place: (half, i, 0, 0))
    if spread:
        product = pl.BlockSpec((step, rows, wide), lambda i, place: (i, 0, 0))
        shape = jax.ShapeDtypeStruct((chips, rows, wide), BF16)
    else:
        product = pl.BlockSpec((ring, step, rows, wide), lambda i, place: (0, i, 0, 0))
        shape = jax.ShapeDtypeStruct((ring, chips, rows, wide), BF16)
    grads = jax.ShapeDtypeStruct((2, chips, share, units), BF16)
    return pl.pallas_call(
        functools.partial(back_kernel, spread=count),
        grid_spec=pltpu.PrefetchScalarGridSpec(
            num_scalar_prefetch=1,
            grid=(2,),
            in_specs=[chunk, stash, stash] + [fixed] * 4 + [pl.BlockSpec(memory_space=pl.ANY)] * len(before),
            out_specs=[wanted, wanted] + [product] * count,
            scratch_shapes=[pltpu.VMEM((step, ring, rows, wide), F32)],
        ),
        out_shape=[grads, grads] + [shape] * count,
        input_output_aliases={8 + i: i for i in range(len(before))},
        compiler_params=pltpu.CompilerParams(vmem_limit_bytes=36 * 2**20),
        cost_estimate=pl.CostEstimate(
            flops=4 * chips * share * units * wide, bytes_accessed=10 * 2**20, transcendentals=grad.size
        ),
    )(place, grad, gate, up, *weights, *before)


def contract_rows(left, right):
    return lax.dot_general(left, right, (((0,), (0,)), ((), ())), preferred_element_type=F32)


def against_weight(left, weight):
    return lax.dot_general(left, weight, (((1,), (1,)), ((), ())), preferred_element_type=F32)


def part_kernel(place, grad, near_own, near_other, far_own, far_other, out):
    narrow = near_own.shape[1]
    shape = out.shape[0], out.shape[2], out.shape[3]
    for flip, (own, other) in enumerate(((near_own, near_other), (far_own, far_other))):
        value = against_weight(grad[:, :narrow], own[...]) + against_weight(grad[:, narrow:], other[...])
        out[:, place[0] ^ flip] = value.astype(BF16).reshape(shape)


def partial_product(x_lo, grad, weights, chips):
    tokens, units = grad.shape[0], weights[0].shape[0]
    vmem = pl.BlockSpec(memory_space=pltpu.VMEM)
    return pl.pallas_call(
        part_kernel,
        out_shape=jax.ShapeDtypeStruct((chips, 2, tokens // chips, units), BF16),
        in_specs=[pl.BlockSpec(memory_space=pltpu.SMEM)] + [vmem] * 5,
        out_specs=vmem,
        compiler_params=pltpu.CompilerParams(vmem_limit_bytes=28 * 2**20),
        cost_estimate=pl.CostEstimate(flops=4 * tokens * units * grad.shape[1], bytes_accessed=7 * 2**20, transcendentals=0),
    )(x_lo.reshape(1), grad, *weights)


def shards(inputs, out_grad, gate_pre, up_pre, gate_weight, up_weight, down_weight):
    core, x_lo = lax.axis_index("c"), lax.axis_index("xl")
    rows = inputs.shape[0]
    chips = lax.axis_size(CHIPS)
    ring = lax.axis_size("z")
    wide = inputs.shape[1] // chips
    narrow = wide // 2
    share, units = gate_pre.shape
    tokens = chips * share

    def by_chip(value):
        return value.reshape(rows, chips, wide).transpose(1, 0, 2)

    gate_all = lax.all_gather(gate_pre, CHIPS, axis=0, tiled=True)

    both = jnp.concatenate([by_chip(out_grad), by_chip(inputs)], axis=1)
    both = lax.all_to_all(both, CHIPS, split_axis=0, concat_axis=0, tiled=True)
    both = jnp.where(core == 0, both, jnp.roll(both, narrow, axis=2))
    both_far = swap(both, "xl")

    down_far = swap(down_weight, "xl")
    down_pieces = (down_weight, swap(down_weight, "c"), down_far, swap(down_far, "c"))
    back_pieces = (gate_weight, swap(gate_weight, "c"), up_weight, swap(up_weight, "c"))

    def spread(value):
        value = jnp.broadcast_to(value[None], (chips, *value.shape))
        value = lax.all_to_all(value, CHIPS, split_axis=0, concat_axis=0, tiled=True)
        return value.reshape(tokens, units)

    up_all = spread(up_pre)

    near_grad, _ = ring_gather(both[:, :rows])[0]()
    part = partial_product(x_lo, near_grad.reshape(tokens // 2, wide), down_pieces, chips)
    part, both_far, up_all, *back_pieces = lax.optimization_barrier((part, both_far, up_all, *back_pieces))
    part = part.reshape(2 * chips, share // 2, units)
    part = lax.all_to_all(part, PLANE, split_axis=0, concat_axis=0, tiled=True)

    second = jnp.concatenate([both_far, both[:, rows:]], axis=1)
    last, landed = ring_gather(second)
    part, landed[2] = lax.optimization_barrier((part, landed[2]))
    part = part.reshape(chips, 2, share // 2, units)

    def across(value, axis):
        return lax.all_to_all(value, axis, split_axis=0, concat_axis=0, tiled=True)

    far_hidden = sum_and_copy(part, 1 - x_lo)
    part, far_hidden, gate_all = lax.optimization_barrier((part, far_hidden, gate_all))
    near_hidden = sum_and_copy(part, x_lo)
    near_hidden, gate_all = lax.optimization_barrier((near_hidden, gate_all))

    def halves(value):
        value = value.reshape(chips, 2, share // 2, units)
        picked = [lax.dynamic_index_in_dim(value, i, axis=1, keepdims=False) for i in (1 - x_lo, x_lo)]
        return jnp.stack(picked).reshape(tokens, units).astype(F32)

    gate_values = halves(gate_all)
    hidden = (gate_values * jax.nn.sigmoid(gate_values) * halves(up_all)).astype(BF16)

    near_hidden, hidden = lax.optimization_barrier((near_hidden, hidden))
    far_hidden, near_hidden = across(far_hidden, CHIPS), across(near_hidden, CHIPS)

    def other(left, right):
        return swap(contract_rows(left, right).astype(BF16), "c")

    def finish(left, right, landed):
        return contract_rows(left, right) + landed.astype(F32)

    gate_all, up_all = (value.reshape(chips, 2, share // 2, units) for value in (gate_all, up_all))
    z = lax.axis_index("z")
    grad_gate, grad_up, *far_parts = swiglu_back(
        jnp.stack([1 - x_lo, z]), 0, far_hidden, gate_all, up_all, back_pieces, (), wide, rows, True
    )
    far_parts[3:6] = [shift(far_parts[k], "z", k) for k in (3, 4, 5)]
    second, far_parts[0] = last(far_parts[0])
    near_hidden, second, far_parts = lax.optimization_barrier((near_hidden, second, far_parts))

    def join(near, far):
        return jnp.stack([far, near]).reshape(tokens, wide)

    grad_cols = join(near_grad, second[:, :, :rows])
    in_cols = join(second[:, :, 2 * rows :], second[:, :, rows : 2 * rows])
    for k in (1, 2, 6, 7):
        far_parts[k] = shift(far_parts[k], "z", k)
    grad_gate, grad_up, near_part = swiglu_back(
        jnp.stack([x_lo, z]), 1, near_hidden, gate_all, up_all, back_pieces, (grad_gate, grad_up), wide, rows, False
    )
    near_part = across(near_part, "z")
    far_sum = swap(sum(part.astype(F32) for part in far_parts).astype(BF16), "xl")
    summed = (jnp.sum(near_part.astype(F32), axis=0) + far_sum.astype(F32)).astype(BF16)
    mine, theirs = summed[:, :, :narrow], swap(summed[:, :, narrow:], "c")
    first, second = jnp.where(core == 0, mine, theirs), jnp.where(core == 0, theirs, mine)
    input_grad = jnp.stack([first, second], axis=1).reshape(2 * chips, rows, narrow)

    grad_gate, grad_up = grad_gate.reshape(tokens, units), grad_up.reshape(tokens, units)
    gate_other, up_other = other(in_cols[:, narrow:], grad_gate), other(in_cols[:, narrow:], grad_up)
    down_other = other(hidden, grad_cols[:, narrow:])
    down_grad = finish(hidden, grad_cols[:, :narrow], down_other)
    gate_grad = finish(in_cols[:, :narrow], grad_gate, gate_other)
    up_grad = finish(in_cols[:, :narrow], grad_up, up_other)
    return (input_grad, gate_grad, up_grad, down_grad)


def solution(mesh):
    grid = Mesh(mesh.devices.reshape(2, 4, 2, 2, 8), ("xh", "y", "c", "xl", "z"))
    dp, tensor = ("xh", "y", "c"), ("xl", "z")
    in_specs = (
        P(dp + tensor, None),
        P(dp + tensor, None),
        P(dp, tensor),
        P(dp, tensor),
        P(dp, tensor),
        P(dp, tensor),
        P(tensor, dp),
    )
    out_specs = (P(None, tensor, dp), P(dp, tensor), P(dp, tensor), P(tensor, dp))
    return jax.shard_map(shards, mesh=grid, in_specs=in_specs, out_specs=out_specs, check_vma=False)
```

```python
import jax
import jax.numpy as jnp
from jax import lax
from jax.experimental import pallas as pl
from jax.experimental.pallas import tpu as pltpu
from jax.sharding import Mesh, PartitionSpec as P

BF16 = jnp.bfloat16
F32 = jnp.float32
CHIPS = ("xh", "y")
PLANE = ("xh", "y", "xl")


def swap(value, axis):
    return lax.ppermute(value, axis, [(0, 1), (1, 0)])


def shift(value, axis, by):
    size = lax.axis_size(axis)
    return lax.ppermute(value, axis, [(i, (i + by) % size) for i in range(size)])


def ring_gather(own, given=None):
    z = lax.axis_index("z")
    chips, rows, wide = own.shape
    half = chips // 2
    whole = jnp.zeros((chips, 8, rows, wide), own.dtype)

    def put(whole, block, by, first=0):
        place = lax.rem(z + by + 8, 8)
        return lax.dynamic_update_slice(whole, block[:, None], (first, place, 0, 0))

    whole = put(whole, own, 0)
    right = left = own
    for by in range(1, 4):
        right, left = shift(right, "z", 1), shift(left, "z", -1)
        whole = put(put(whole, right, -by), left, by)

    if given is not None:
        whole, given = lax.optimization_barrier((whole, given))
    right, left = shift(right[:half], "z", 1), shift(left[half:], "z", -1)
    return put(put(whole, right, 4), left, 4, half), given


def beside(send, job, *given):
    send, given = lax.optimization_barrier((send, given))
    landed = (shift(send[0], "z", 1), shift(send[1], "z", -1))
    return lax.optimization_barrier((landed, job(*given)))


def ring_scatter(blocks, jobs, given):
    z = lax.axis_index("z")
    half = blocks.shape[0] // 2

    def block(k):
        return lax.dynamic_index_in_dim(blocks, lax.rem(z + k, 8), axis=2, keepdims=False)

    far = block(4).astype(BF16)
    (right, left), state = beside((far[:half], far[half:]), jobs[0], *given)
    for k, job in zip((3, 2, 1), jobs[1:]):
        mine, other = block(k), block(8 - k)
        if k == 3:
            mine = jnp.concatenate([mine[:half] + right.astype(F32), mine[half:]], axis=0)
            other = jnp.concatenate([other[:half], other[half:] + left.astype(F32)], axis=0)
        else:
            mine = mine + right.astype(F32)
            other = other + left.astype(F32)
        if k > 1:
            mine, other = mine.astype(BF16), other.astype(BF16)
        (right, left), state = beside((mine, other), job, *state)
    return block(0) + right + left, state


def sum_kernel(parts, out):
    total = jnp.sum(parts[...].astype(F32), axis=0).astype(BF16)
    for i in range(out.shape[0]):
        out[i] = total


def sum_and_copy(parts):
    count, rows, units = parts.shape
    step = rows // 4
    spec = pl.BlockSpec((count, step, units), lambda i: (0, i, 0))
    return pl.pallas_call(
        sum_kernel,
        grid=(4,),
        out_shape=jax.ShapeDtypeStruct(parts.shape, BF16),
        in_specs=[spec],
        out_specs=spec,
        compiler_params=pltpu.CompilerParams(vmem_limit_bytes=56 * 2**20),
        cost_estimate=pl.CostEstimate(flops=parts.size, bytes_accessed=4 * parts.size, transcendentals=0),
    )(parts)


def back_kernel(grad, gate, up, gate_own, gate_other, up_own, up_other, grad_gate, grad_up, near, far):
    narrow = gate_own.shape[0]
    halves, ring, chips, rows, _ = far.shape
    gate_values, up_values = gate[...].astype(F32), up[...].astype(F32)
    grad_hidden = grad[...].astype(F32)
    sigmoid = jax.nn.sigmoid(gate_values)
    slope = sigmoid * (1.0 + gate_values * (1.0 - sigmoid))
    left = (grad_hidden * up_values * slope).astype(BF16)
    right = (grad_hidden * (gate_values * sigmoid)).astype(BF16)
    grad_gate[...], grad_up[...] = left, right
    value = against_weight(left, gate_other[...]) + against_weight(right, up_other[...])
    value = value.reshape(chips, halves, ring, rows, narrow)
    for chip in range(chips):
        far[:, :, chip] = value[chip].astype(BF16)
    near[...] = against_weight(left, gate_own[...]) + against_weight(right, up_own[...])


def swiglu_back(grad, gate, up, weights, ring, rows):
    tokens, units = grad.shape
    narrow = weights[0].shape[0]
    chips = tokens // (2 * ring * rows)
    step = 2 * (2 * ring * rows)
    moving = pl.BlockSpec((step, units), lambda i: (i, 0))
    fixed = pl.BlockSpec(weights[0].shape, lambda i: (0, 0))
    return pl.pallas_call(
        back_kernel,
        grid=(tokens // step,),
        out_shape=(
            jax.ShapeDtypeStruct((tokens, units), BF16),
            jax.ShapeDtypeStruct((tokens, units), BF16),
            jax.ShapeDtypeStruct((tokens, narrow), F32),
            jax.ShapeDtypeStruct((2, ring, chips, rows, narrow), BF16),
        ),
        in_specs=[moving] * 3 + [fixed] * 4,
        out_specs=(
            moving,
            moving,
            pl.BlockSpec((step, narrow), lambda i: (i, 0)),
            pl.BlockSpec((2, ring, 2, rows, narrow), lambda i: (0, 0, i, 0, 0)),
        ),
        compiler_params=pltpu.CompilerParams(vmem_limit_bytes=56 * 2**20),
        cost_estimate=pl.CostEstimate(
            flops=8 * tokens * units * narrow, bytes_accessed=17 * 2**20, transcendentals=tokens * units
        ),
    )(grad, gate, up, *weights)


def contract_rows(left, right):
    return lax.dot_general(left, right, (((0,), (0,)), ((), ())), preferred_element_type=F32)


def against_weight(left, weight):
    return lax.dot_general(left, weight, (((1,), (1,)), ((), ())), preferred_element_type=F32)


def part_kernel(place, grad, near_own, near_other, far_own, far_other, out):
    narrow = near_own.shape[1]
    shape = out.shape[0], out.shape[2], out.shape[3]
    for flip, (own, other) in enumerate(((near_own, near_other), (far_own, far_other))):
        value = against_weight(grad[:, :narrow], own[...]) + against_weight(grad[:, narrow:], other[...])
        out[:, place[0] ^ flip] = value.astype(BF16).reshape(shape)


def partial_product(x_lo, grad, weights, chips):
    tokens, units = grad.shape[0], weights[0].shape[0]
    vmem = pl.BlockSpec(memory_space=pltpu.VMEM)
    return pl.pallas_call(
        part_kernel,
        out_shape=jax.ShapeDtypeStruct((chips, 2, tokens // chips, units), BF16),
        in_specs=[pl.BlockSpec(memory_space=pltpu.SMEM)] + [vmem] * 5,
        out_specs=vmem,
        compiler_params=pltpu.CompilerParams(vmem_limit_bytes=56 * 2**20),
        cost_estimate=pl.CostEstimate(flops=4 * tokens * units * grad.shape[1], bytes_accessed=7 * 2**20, transcendentals=0),
    )(x_lo.reshape(1), grad, *weights)


def shards(inputs, out_grad, gate_pre, up_pre, gate_weight, up_weight, down_weight):
    core, x_lo = lax.axis_index("c"), lax.axis_index("xl")
    rows = inputs.shape[0]
    chips = lax.axis_size(CHIPS)
    ring = lax.axis_size("z")
    wide = inputs.shape[1] // chips
    narrow = wide // 2
    share, units = gate_pre.shape
    tokens = chips * share

    def by_chip(value):
        return value.reshape(rows, chips, wide).transpose(1, 0, 2)

    gate_all = lax.all_gather(gate_pre, CHIPS, axis=0, tiled=True)

    both = jnp.concatenate([by_chip(out_grad), by_chip(inputs)], axis=1)
    both = lax.all_to_all(both, CHIPS, split_axis=0, concat_axis=0, tiled=True)
    both = jnp.where(core == 0, both, jnp.roll(both, narrow, axis=2))
    both_far = swap(both, "xl")

    down_far = swap(down_weight, "xl")
    down_pieces = (down_weight, swap(down_weight, "c"), down_far, swap(down_far, "c"))
    back_pieces = (gate_weight, swap(gate_weight, "c"), up_weight, swap(up_weight, "c"))

    def spread(value):
        value = jnp.broadcast_to(value[None], (chips, *value.shape))
        value = lax.all_to_all(value, CHIPS, split_axis=0, concat_axis=0, tiled=True)
        return value.reshape(tokens, units)

    up_all = spread(up_pre)

    near_grad, _ = ring_gather(both[:, :rows])
    part = partial_product(x_lo, near_grad.reshape(tokens // 2, wide), down_pieces, chips)
    part, up_all, own_in, *back_pieces = lax.optimization_barrier((part, up_all, both[:, rows:], *back_pieces))
    part = part.reshape(2 * chips, share // 2, units)
    part = lax.all_to_all(part, PLANE, split_axis=0, concat_axis=0, tiled=True)

    second, part = ring_gather(jnp.concatenate([both_far, own_in], axis=1), part)
    grad_hidden = sum_and_copy(part.reshape(chips, share, units))
    grad_hidden, gate_all = lax.optimization_barrier((grad_hidden, gate_all))
    grad_hidden = lax.all_to_all(grad_hidden, CHIPS, split_axis=0, concat_axis=0, tiled=True)
    grad_hidden = grad_hidden.reshape(tokens, units)

    def join(near, far):
        pair = jnp.where(x_lo == 0, jnp.stack([near, far], 1), jnp.stack([far, near], 1))
        return pair.reshape(tokens, wide)

    grad_cols = join(near_grad, second[:, :, :rows])
    in_cols = join(second[:, :, 2 * rows :], second[:, :, rows : 2 * rows])
    gate_values = gate_all.astype(F32)
    hidden = (gate_values * jax.nn.sigmoid(gate_values) * up_all.astype(F32)).astype(BF16)

    def finish(left, right, landed):
        return contract_rows(left, right) + landed.astype(F32)

    down_grad = finish(
        hidden, grad_cols[:, :narrow], swap(contract_rows(hidden, grad_cols[:, narrow:]).astype(BF16), "c")
    )
    grad_hidden, in_cols, down_grad = lax.optimization_barrier((grad_hidden, in_cols, down_grad))
    grad_gate, grad_up, near_part, far_part = swiglu_back(grad_hidden, gate_all, up_all, back_pieces, ring, rows)

    far_part = far_part.reshape(2 * ring, chips, rows, narrow)
    far_part = lax.all_to_all(far_part, ("xl", "z"), split_axis=0, concat_axis=0, tiled=True)
    def others(*values):
        return tuple(contract_rows(in_cols[:, narrow:], value).astype(BF16) for value in values)

    moving = []

    def send_others(*values):
        moving.extend(swap(value, "c") for value in values)
        return values

    jobs = (lambda *values: values, others, send_others, lambda *values: (*moving, far_part))
    summed, (gate_other, up_other, far_part) = ring_scatter(
        near_part.reshape(chips, 2, ring, rows, narrow), jobs, (grad_gate, grad_up)
    )
    far_part = swap(jnp.sum(far_part.astype(F32), axis=0).astype(BF16), "c")
    mine, theirs = (
        lax.dynamic_index_in_dim(summed, place, axis=1, keepdims=False) for place in (x_lo, 1 - x_lo)
    )
    mine = (mine + swap(theirs, "xl")).astype(BF16)
    first, second = jnp.where(core == 0, mine, far_part), jnp.where(core == 0, far_part, mine)
    input_grad = jnp.stack([first, second], axis=1).reshape(2 * chips, rows, narrow)

    gate_grad = finish(in_cols[:, :narrow], grad_gate, gate_other)
    up_grad = finish(in_cols[:, :narrow], grad_up, up_other)
    return (input_grad, gate_grad, up_grad, down_grad)


def solution(mesh):
    grid = Mesh(mesh.devices.reshape(2, 4, 2, 2, 8), ("xh", "y", "c", "xl", "z"))
    dp, tensor = ("xh", "y", "c"), ("xl", "z")
    in_specs = (
        P(dp + tensor, None),
        P(dp + tensor, None),
        P(dp, tensor),
        P(dp, tensor),
        P(dp, tensor),
        P(dp, tensor),
        P(tensor, dp),
    )
    out_specs = (P(None, tensor, dp), P(dp, tensor), P(dp, tensor), P(tensor, dp))
    return jax.shard_map(shards, mesh=grid, in_specs=in_specs, out_specs=out_specs, check_vma=False)
```

```python
import jax
import jax.numpy as jnp
from jax import lax
from jax.experimental import pallas as pl
from jax.experimental.pallas import tpu as pltpu
from jax.sharding import Mesh, PartitionSpec as P

BF16 = jnp.bfloat16
F32 = jnp.float32
CHIPS = ("xh", "y")
PLANE = ("xh", "y", "xl")


def swap(value, axis):
    return lax.ppermute(value, axis, [(0, 1), (1, 0)])


def shift(value, axis, by):
    size = lax.axis_size(axis)
    return lax.ppermute(value, axis, [(i, (i + by) % size) for i in range(size)])


def after(value, *others):
    return lax.optimization_barrier((value, *others))[0]


def ring_gather(own):
    z = lax.axis_index("z")
    chips, rows, wide = own.shape
    half = chips // 2
    whole = jnp.zeros((chips, 8, rows, wide), own.dtype)

    def put(whole, block, by, first=0):
        place = lax.rem(z + by + 8, 8)
        return lax.dynamic_update_slice(whole, block[:, None], (first, place, 0, 0))

    whole = put(whole, own, 0)
    right = left = own
    landed = []
    for by in range(1, 4):
        right, left = shift(right, "z", 1), shift(left, "z", -1)
        whole = put(put(whole, right, -by), left, by)
        landed.append((right, left))

    def last(*hold):
        (right, left), _ = lax.optimization_barrier((landed[-1], hold))
        right, left = shift(right[:half], "z", 1), shift(left[half:], "z", -1)
        return put(put(whole, right, 4), left, 4, half)

    return last, landed


def beside(send, job, *given):
    send, given = lax.optimization_barrier((send, given))
    landed = (shift(send[0], "z", 1), shift(send[1], "z", -1))
    return lax.optimization_barrier((landed, job(*given)))


def ring_scatter(blocks, jobs, given):
    z = lax.axis_index("z")
    half = blocks.shape[0] // 2

    def block(k):
        return lax.dynamic_index_in_dim(blocks, lax.rem(z + k, 8), axis=2, keepdims=False)

    far = block(4).astype(BF16)
    (right, left), state = beside((far[:half], far[half:]), jobs[0], *given)
    for k, job in zip((3, 2, 1), jobs[1:]):
        mine, other = block(k), block(8 - k)
        if k == 3:
            mine = jnp.concatenate([mine[:half] + right.astype(F32), mine[half:]], axis=0)
            other = jnp.concatenate([other[:half], other[half:] + left.astype(F32)], axis=0)
        else:
            mine = mine + right.astype(F32)
            other = other + left.astype(F32)
        if k > 1:
            mine, other = mine.astype(BF16), other.astype(BF16)
        (right, left), state = beside((mine, other), job, *state)
    return block(0) + right + left, state


def sum_kernel(parts, out):
    total = jnp.sum(parts[...].astype(F32), axis=0).astype(BF16)
    for i in range(out.shape[0]):
        out[i] = total


def sum_and_copy(parts):
    count, rows, units = parts.shape
    step = rows // 4
    spec = pl.BlockSpec((count, step, units), lambda i: (0, i, 0))
    return pl.pallas_call(
        sum_kernel,
        grid=(4,),
        out_shape=jax.ShapeDtypeStruct(parts.shape, BF16),
        in_specs=[spec],
        out_specs=spec,
        compiler_params=pltpu.CompilerParams(vmem_limit_bytes=56 * 2**20),
        cost_estimate=pl.CostEstimate(flops=parts.size, bytes_accessed=4 * parts.size, transcendentals=0),
    )(parts)


def back_kernel(grad, gate_slope, up_slope, gate_own, gate_other, up_own, up_other, grad_gate, grad_up, out):
    narrow = gate_own.shape[0]
    grad_hidden = grad[...].astype(F32)
    left = (grad_hidden * gate_slope[...]).astype(BF16)
    right = (grad_hidden * up_slope[...]).astype(BF16)
    grad_gate[...], grad_up[...] = left, right
    out[:, :narrow] = against_weight(left, gate_own[...]) + against_weight(right, up_own[...])
    out[:, narrow:] = against_weight(left, gate_other[...]) + against_weight(right, up_other[...])


def swiglu_back(grad, gate_slope, up_slope, weights, wide):
    tokens, units = grad.shape
    step = min(256, tokens)
    moving = pl.BlockSpec((step, units), lambda i: (i, 0))
    fixed = pl.BlockSpec(weights[0].shape, lambda i: (0, 0))
    return pl.pallas_call(
        back_kernel,
        grid=(tokens // step,),
        out_shape=(
            jax.ShapeDtypeStruct((tokens, units), BF16),
            jax.ShapeDtypeStruct((tokens, units), BF16),
            jax.ShapeDtypeStruct((tokens, wide), F32),
        ),
        in_specs=[moving] * 3 + [fixed] * 4,
        out_specs=(moving, moving, pl.BlockSpec((step, wide), lambda i: (i, 0))),
        compiler_params=pltpu.CompilerParams(vmem_limit_bytes=56 * 2**20),
        cost_estimate=pl.CostEstimate(flops=4 * tokens * units * wide, bytes_accessed=22 * 2**20, transcendentals=0),
    )(grad, gate_slope, up_slope, *weights)


def contract_rows(left, right):
    return lax.dot_general(left, right, (((0,), (0,)), ((), ())), preferred_element_type=F32)


def against_weight(left, weight):
    return lax.dot_general(left, weight, (((1,), (1,)), ((), ())), preferred_element_type=F32)


def part_kernel(place, grad, near_own, near_other, far_own, far_other, out):
    narrow = near_own.shape[1]
    shape = out.shape[0], out.shape[2], out.shape[3]
    for flip, (own, other) in enumerate(((near_own, near_other), (far_own, far_other))):
        value = against_weight(grad[:, :narrow], own[...]) + against_weight(grad[:, narrow:], other[...])
        out[:, place[0] ^ flip] = value.astype(BF16).reshape(shape)


def partial_product(x_lo, grad, weights, chips):
    tokens, units = grad.shape[0], weights[0].shape[0]
    vmem = pl.BlockSpec(memory_space=pltpu.VMEM)
    return pl.pallas_call(
        part_kernel,
        out_shape=jax.ShapeDtypeStruct((chips, 2, tokens // chips, units), BF16),
        in_specs=[pl.BlockSpec(memory_space=pltpu.SMEM)] + [vmem] * 5,
        out_specs=vmem,
        compiler_params=pltpu.CompilerParams(vmem_limit_bytes=56 * 2**20),
        cost_estimate=pl.CostEstimate(flops=4 * tokens * units * grad.shape[1], bytes_accessed=7 * 2**20, transcendentals=0),
    )(x_lo.reshape(1), grad, *weights)


def shards(inputs, out_grad, gate_pre, up_pre, gate_weight, up_weight, down_weight):
    core, x_lo = lax.axis_index("c"), lax.axis_index("xl")
    rows = inputs.shape[0]
    chips = lax.axis_size(CHIPS)
    ring = lax.axis_size("z")
    wide = inputs.shape[1] // chips
    narrow = wide // 2
    share, units = gate_pre.shape
    tokens = chips * share

    def by_chip(value):
        return value.reshape(rows, chips, wide).transpose(1, 0, 2)

    gate_all = lax.all_gather(gate_pre, CHIPS, axis=0, tiled=True)

    both = jnp.concatenate([by_chip(out_grad), by_chip(inputs)], axis=1)
    both = lax.all_to_all(both, CHIPS, split_axis=0, concat_axis=0, tiled=True)
    both = jnp.where(core == 0, both, jnp.roll(both, narrow, axis=2))
    both_far = swap(both, "xl")

    down_far = swap(down_weight, "xl")
    down_pieces = (down_weight, swap(down_weight, "c"), down_far, swap(down_far, "c"))
    back_pieces = (gate_weight, swap(gate_weight, "c"), up_weight, swap(up_weight, "c"))

    def spread(value):
        value = jnp.broadcast_to(value[None], (chips, *value.shape))
        value = lax.all_to_all(value, CHIPS, split_axis=0, concat_axis=0, tiled=True)
        return value.reshape(tokens, units)

    up_all = spread(after(up_pre, both))

    near_grad = ring_gather(both[:, :rows])[0]()
    part = partial_product(x_lo, near_grad.reshape(tokens // 2, wide), down_pieces, chips)
    part, up_all, *back_pieces = lax.optimization_barrier((part, up_all, *back_pieces))
    sent = part = part.reshape(2 * chips, share // 2, units)
    part = lax.all_to_all(part, PLANE, split_axis=0, concat_axis=0, tiled=True)

    second = jnp.concatenate([after(both_far, sent), both[:, rows:]], axis=1)
    last, landed = ring_gather(second)
    part, landed[1] = lax.optimization_barrier((part, landed[1]))
    grad_hidden = sum_and_copy(part.reshape(chips, share, units))
    grad_hidden, gate_all = lax.optimization_barrier((grad_hidden, gate_all))
    second = last(grad_hidden)
    grad_hidden = lax.all_to_all(grad_hidden, CHIPS, split_axis=0, concat_axis=0, tiled=True)
    grad_hidden = grad_hidden.reshape(tokens, units)

    def join(near, far):
        pair = jnp.where(x_lo == 0, jnp.stack([near, far], 1), jnp.stack([far, near], 1))
        return pair.reshape(tokens, wide)

    grad_cols = join(near_grad, second[:, :, :rows])
    in_cols = join(second[:, :, 2 * rows :], second[:, :, rows : 2 * rows])
    gate_values, up_values = gate_all.astype(F32), up_all.astype(F32)
    sigmoid = jax.nn.sigmoid(gate_values)
    up_slope = gate_values * sigmoid
    gate_slope = up_values * sigmoid * (1.0 + gate_values * (1.0 - sigmoid))
    hidden = (up_slope * up_values).astype(BF16)

    def finish(left, right, landed):
        return contract_rows(left, right) + landed.astype(F32)

    down_grad = finish(
        hidden, grad_cols[:, :narrow], swap(contract_rows(hidden, grad_cols[:, narrow:]).astype(BF16), "c")
    )
    grad_hidden, gate_slope, up_slope, in_cols, down_grad = lax.optimization_barrier(
        (grad_hidden, gate_slope, up_slope, in_cols, down_grad)
    )
    grad_gate, grad_up, in_part = swiglu_back(grad_hidden, gate_slope, up_slope, back_pieces, wide)

    def others(*values):
        return tuple(contract_rows(in_cols[:, narrow:], value).astype(BF16) for value in values)

    moving = []

    def send_others(*values):
        moving.extend(swap(value, "c") for value in values)
        return values

    jobs = (
        lambda *values: values,
        others,
        send_others,
        lambda *values: (finish(in_cols[:, :narrow], grad_gate, moving[0]), moving[1]),
    )
    summed, (gate_grad, up_grad) = ring_scatter(in_part.reshape(chips, 2, ring, rows, wide), jobs, (grad_gate, grad_up))
    up_grad = finish(in_cols[:, :narrow], grad_up, up_grad)
    mine, theirs = (
        lax.dynamic_index_in_dim(summed, place, axis=1, keepdims=False) for place in (x_lo, 1 - x_lo)
    )
    summed = (mine + swap(theirs, "xl")).astype(BF16)
    mine, theirs = summed[:, :, :narrow], swap(summed[:, :, narrow:], "c")
    first, second = jnp.where(core == 0, mine, theirs), jnp.where(core == 0, theirs, mine)
    input_grad = jnp.stack([first, second], axis=1).reshape(2 * chips, rows, narrow)
    return (input_grad, gate_grad, up_grad, down_grad)


def solution(mesh):
    grid = Mesh(mesh.devices.reshape(2, 4, 2, 2, 8), ("xh", "y", "c", "xl", "z"))
    dp, tensor = ("xh", "y", "c"), ("xl", "z")
    in_specs = (
        P(dp + tensor, None),
        P(dp + tensor, None),
        P(dp, tensor),
        P(dp, tensor),
        P(dp, tensor),
        P(dp, tensor),
        P(tensor, dp),
    )
    out_specs = (P(None, tensor, dp), P(dp, tensor), P(dp, tensor), P(tensor, dp))
    return jax.shard_map(shards, mesh=grid, in_specs=in_specs, out_specs=out_specs, check_vma=False)
```

```python
import jax
import jax.numpy as jnp
from jax import lax
from jax.experimental import pallas as pl
from jax.experimental.pallas import tpu as pltpu
from jax.sharding import Mesh, PartitionSpec as P

BF16 = jnp.bfloat16
F32 = jnp.float32
CHIPS = ("xh", "y")
PLANE = ("xh", "y", "xl")


def swap(value, axis):
    return lax.ppermute(value, axis, [(0, 1), (1, 0)])


def shift(value, axis, by):
    size = lax.axis_size(axis)
    return lax.ppermute(value, axis, [(i, (i + by) % size) for i in range(size)])


def after(value, *others):
    return lax.optimization_barrier((value, *others))[0]


def ring_gather(own):
    z = lax.axis_index("z")
    chips, rows, wide = own.shape
    half = chips // 2
    whole = jnp.zeros((chips, 8, rows, wide), own.dtype)

    def put(whole, block, by, first=0):
        place = lax.rem(z + by + 8, 8)
        return lax.dynamic_update_slice(whole, block[:, None], (first, place, 0, 0))

    whole = put(whole, own, 0)
    right = left = own
    landed = []
    for by in range(1, 4):
        right, left = shift(right, "z", 1), shift(left, "z", -1)
        whole = put(put(whole, right, -by), left, by)
        landed.append((right, left))

    def last(*hold):
        (right, left), _ = lax.optimization_barrier((landed[-1], hold))
        right, left = shift(right[:half], "z", 1), shift(left[half:], "z", -1)
        return put(put(whole, right, 4), left, 4, half)

    return last, landed


def beside(send, job, *given):
    send, given = lax.optimization_barrier((send, given))
    landed = (shift(send[0], "z", 1), shift(send[1], "z", -1))
    return lax.optimization_barrier((landed, job(*given)))


def ring_scatter(blocks, jobs, given):
    z = lax.axis_index("z")
    half = blocks.shape[0] // 2

    def block(k):
        return lax.dynamic_index_in_dim(blocks, lax.rem(z + k, 8), axis=2, keepdims=False)

    far = block(4).astype(BF16)
    (right, left), state = beside((far[:half], far[half:]), jobs[0], *given)
    for k, job in zip((3, 2, 1), jobs[1:]):
        mine, other = block(k), block(8 - k)
        if k == 3:
            mine = jnp.concatenate([mine[:half] + right.astype(F32), mine[half:]], axis=0)
            other = jnp.concatenate([other[:half], other[half:] + left.astype(F32)], axis=0)
        else:
            mine = mine + right.astype(F32)
            other = other + left.astype(F32)
        if k > 1:
            mine, other = mine.astype(BF16), other.astype(BF16)
        (right, left), state = beside((mine, other), job, *state)
    return block(0) + right + left, state


def sum_kernel(parts, out):
    total = jnp.sum(parts[...].astype(F32), axis=0).astype(BF16)
    for i in range(out.shape[0]):
        out[i] = total


def sum_and_copy(parts):
    count, rows, units = parts.shape
    step = rows // 4
    spec = pl.BlockSpec((count, step, units), lambda i: (0, i, 0))
    return pl.pallas_call(
        sum_kernel,
        grid=(4,),
        out_shape=jax.ShapeDtypeStruct(parts.shape, BF16),
        in_specs=[spec],
        out_specs=spec,
        compiler_params=pltpu.CompilerParams(vmem_limit_bytes=24 * 2**20),
        cost_estimate=pl.CostEstimate(flops=parts.size, bytes_accessed=4 * parts.size, transcendentals=0),
    )(parts)


def back_kernel(grad, gate_slope, up_slope, gate_own, gate_other, up_own, up_other, grad_gate, grad_up, out):
    narrow = gate_own.shape[0]
    grad_hidden = grad[...].astype(F32)
    left = (grad_hidden * gate_slope[...]).astype(BF16)
    right = (grad_hidden * up_slope[...]).astype(BF16)
    grad_gate[...], grad_up[...] = left, right
    out[:, :narrow] = against_weight(left, gate_own[...]) + against_weight(right, up_own[...])
    out[:, narrow:] = against_weight(left, gate_other[...]) + against_weight(right, up_other[...])


def swiglu_back(grad, gate_slope, up_slope, weights, wide):
    tokens, units = grad.shape
    step = min(256, tokens)
    moving = pl.BlockSpec((step, units), lambda i: (i, 0))
    fixed = pl.BlockSpec(weights[0].shape, lambda i: (0, 0))
    return pl.pallas_call(
        back_kernel,
        grid=(tokens // step,),
        out_shape=(
            jax.ShapeDtypeStruct((tokens, units), BF16),
            jax.ShapeDtypeStruct((tokens, units), BF16),
            jax.ShapeDtypeStruct((tokens, wide), F32),
        ),
        in_specs=[moving] * 3 + [fixed] * 4,
        out_specs=(moving, moving, pl.BlockSpec((step, wide), lambda i: (i, 0))),
        compiler_params=pltpu.CompilerParams(vmem_limit_bytes=56 * 2**20),
        cost_estimate=pl.CostEstimate(flops=4 * tokens * units * wide, bytes_accessed=22 * 2**20, transcendentals=0),
    )(grad, gate_slope, up_slope, *weights)


def contract_rows(left, right):
    return lax.dot_general(left, right, (((0,), (0,)), ((), ())), preferred_element_type=F32)


def against_weight(left, weight):
    return lax.dot_general(left, weight, (((1,), (1,)), ((), ())), preferred_element_type=F32)


def part_kernel(place, grad, near_own, near_other, far_own, far_other, out):
    narrow = near_own.shape[1]
    shape = out.shape[0], out.shape[2], out.shape[3]
    for flip, (own, other) in enumerate(((near_own, near_other), (far_own, far_other))):
        value = against_weight(grad[:, :narrow], own[...]) + against_weight(grad[:, narrow:], other[...])
        out[:, place[0] ^ flip] = value.astype(BF16).reshape(shape)


def partial_product(x_lo, grad, weights, chips):
    tokens, units = grad.shape[0], weights[0].shape[0]
    vmem = pl.BlockSpec(memory_space=pltpu.VMEM)
    return pl.pallas_call(
        part_kernel,
        out_shape=jax.ShapeDtypeStruct((chips, 2, tokens // chips, units), BF16),
        in_specs=[pl.BlockSpec(memory_space=pltpu.SMEM)] + [vmem] * 5,
        out_specs=vmem,
        compiler_params=pltpu.CompilerParams(vmem_limit_bytes=28 * 2**20),
        cost_estimate=pl.CostEstimate(flops=4 * tokens * units * grad.shape[1], bytes_accessed=7 * 2**20, transcendentals=0),
    )(x_lo.reshape(1), grad, *weights)


def shards(inputs, out_grad, gate_pre, up_pre, gate_weight, up_weight, down_weight):
    core, x_lo = lax.axis_index("c"), lax.axis_index("xl")
    rows = inputs.shape[0]
    chips = lax.axis_size(CHIPS)
    ring = lax.axis_size("z")
    wide = inputs.shape[1] // chips
    narrow = wide // 2
    share, units = gate_pre.shape
    tokens = chips * share

    def by_chip(value):
        return value.reshape(rows, chips, wide).transpose(1, 0, 2)

    gate_all = lax.all_gather(gate_pre, CHIPS, axis=0, tiled=True)

    both = jnp.concatenate([by_chip(out_grad), by_chip(inputs)], axis=1)
    both = lax.all_to_all(both, CHIPS, split_axis=0, concat_axis=0, tiled=True)
    both = jnp.where(core == 0, both, jnp.roll(both, narrow, axis=2))
    both_far = swap(both, "xl")

    down_far = swap(down_weight, "xl")
    down_pieces = (down_weight, swap(down_weight, "c"), down_far, swap(down_far, "c"))
    back_pieces = (gate_weight, swap(gate_weight, "c"), up_weight, swap(up_weight, "c"))

    def spread(value):
        value = jnp.broadcast_to(value[None], (chips, *value.shape))
        value = lax.all_to_all(value, CHIPS, split_axis=0, concat_axis=0, tiled=True)
        return value.reshape(tokens, units)

    up_all = spread(after(up_pre, both))

    near_grad = ring_gather(both[:, :rows])[0]()
    part = partial_product(x_lo, near_grad.reshape(tokens // 2, wide), down_pieces, chips)
    part, up_all, *back_pieces = lax.optimization_barrier((part, up_all, *back_pieces))
    sent = part = part.reshape(2 * chips, share // 2, units)
    part = lax.all_to_all(part, PLANE, split_axis=0, concat_axis=0, tiled=True)

    second = jnp.concatenate([after(both_far, sent), both[:, rows:]], axis=1)
    last, landed = ring_gather(second)
    part, landed[1] = lax.optimization_barrier((part, landed[1]))
    grad_hidden = sum_and_copy(part.reshape(chips, share, units))
    grad_hidden, gate_all = lax.optimization_barrier((grad_hidden, gate_all))
    second = last(grad_hidden)
    grad_hidden = lax.all_to_all(grad_hidden, CHIPS, split_axis=0, concat_axis=0, tiled=True)
    grad_hidden = grad_hidden.reshape(tokens, units)

    def join(near, far):
        pair = jnp.where(x_lo == 0, jnp.stack([near, far], 1), jnp.stack([far, near], 1))
        return pair.reshape(tokens, wide)

    grad_cols = join(near_grad, second[:, :, :rows])
    in_cols = join(second[:, :, 2 * rows :], second[:, :, rows : 2 * rows])
    gate_values, up_values = gate_all.astype(F32), up_all.astype(F32)
    sigmoid = jax.nn.sigmoid(gate_values)
    up_slope = gate_values * sigmoid
    gate_slope = up_values * sigmoid * (1.0 + gate_values * (1.0 - sigmoid))
    hidden = (up_slope * up_values).astype(BF16)

    def finish(left, right, landed):
        return contract_rows(left, right) + landed.astype(F32)

    down_grad = finish(
        hidden, grad_cols[:, :narrow], swap(contract_rows(hidden, grad_cols[:, narrow:]).astype(BF16), "c")
    )
    grad_hidden, gate_slope, up_slope, in_cols, down_grad = lax.optimization_barrier(
        (grad_hidden, gate_slope, up_slope, in_cols, down_grad)
    )
    grad_gate, grad_up, in_part = swiglu_back(grad_hidden, gate_slope, up_slope, back_pieces, wide)

    def others(*values):
        return tuple(contract_rows(in_cols[:, narrow:], value).astype(BF16) for value in values)

    jobs = (
        lambda *values: values,
        others,
        lambda gate, up: (swap(gate, "c"), swap(up, "c")),
        lambda gate, up: (finish(in_cols[:, :narrow], grad_gate, gate), up),
    )
    summed, (gate_grad, up_grad) = ring_scatter(in_part.reshape(chips, 2, ring, rows, wide), jobs, (grad_gate, grad_up))
    up_grad = finish(in_cols[:, :narrow], grad_up, up_grad)
    mine, theirs = (
        lax.dynamic_index_in_dim(summed, place, axis=1, keepdims=False) for place in (x_lo, 1 - x_lo)
    )
    summed = (mine + swap(theirs, "xl")).astype(BF16)
    mine, theirs = summed[:, :, :narrow], swap(summed[:, :, narrow:], "c")
    first, second = jnp.where(core == 0, mine, theirs), jnp.where(core == 0, theirs, mine)
    input_grad = jnp.stack([first, second], axis=1).reshape(2 * chips, rows, narrow)
    return (input_grad, gate_grad, up_grad, down_grad)


def solution(mesh):
    grid = Mesh(mesh.devices.reshape(2, 4, 2, 2, 8), ("xh", "y", "c", "xl", "z"))
    dp, tensor = ("xh", "y", "c"), ("xl", "z")
    in_specs = (
        P(dp + tensor, None),
        P(dp + tensor, None),
        P(dp, tensor),
        P(dp, tensor),
        P(dp, tensor),
        P(dp, tensor),
        P(tensor, dp),
    )
    out_specs = (P(None, tensor, dp), P(dp, tensor), P(dp, tensor), P(tensor, dp))
    return jax.shard_map(shards, mesh=grid, in_specs=in_specs, out_specs=out_specs, check_vma=False)
```
